512 devices in a mesh: batch: 4 (over y), tm: 16 (over x, z_lo), space: 8 (over z_hi, core).
Axes of the slice: x: 4, y: 4, z: 16 (z_hi: 4, z_lo: 4; z = z_hi * 4 + z_lo), core: 2. Of those that a mesh axis runs over, the one named last changes fastest.
Arguments:
- tokens: bfloat16 [64, 1024, 1152], P(('batch', 'tm'), 'space'), parts along dimension 0, may hold values from -6 to 6
- frame_qkv: bfloat16 [1152, 3456], P(None, 'space'), may hold values from -4 to 4
- frame_out: bfloat16 [1152, 1152], P('space'), may hold values from -0.375 to 0.375
- time_qkv: bfloat16 [3456, 1152], P('tm'), may hold values from -4 to 4
- time_out: bfloat16 [1152, 1152], replicated, may hold values from -0.375 to 0.375
- modulation: float32 [8, 3, 1152], P('batch'), parts along dimension 0, may hold values from -4 to 4
Outputs:
- blended: bfloat16 [64, 1024, 1152], P(('batch', 'tm'), 'space'), parts along dimension 0
The draws below stay inside these ranges and needn't reach their ends.
There are 4 independent parts, one for each index of `batch`. The reference program is written for one: setup_inputs(seed, part) draws one part's arguments, and reference() takes and returns one part's arrays. A program takes and returns all parts, laid end to end along the dimension named above; an argument that names none is the same for every part. Nothing has to cross between parts.
All inputs are finite; a program needn't handle non-finite values.
Results may differ from the reference program's by a relative error of at most 0.035.
Values may be sent and summed in bfloat16 or wider, within the bound.
No kernel may reach another device: no remote copies, remote signals or barrier semaphores. Data moves between devices by JAX's collectives and lax.ppermute only.
A program may use at most 64 MiB of HBM per device.

```python
import jax
import jax.numpy as jnp
from jax import lax

D = 1152
HEADS = 16
HD = 72
FRAMES = 16
SPATIAL = 1024
N_SPACE = 8


def normal_table(key, bound_factor):
    deviation = 2.0 * D ** (-0.5)
    return jnp.clip(jax.random.normal(key, (D, HEADS, 3, HD), jnp.float32), -bound_factor, bound_factor) * deviation


def draw_tokens(key, part):
    key = jax.random.fold_in(key, 11)
    values = jnp.clip(jax.random.normal(key, (FRAMES, SPATIAL, D), jnp.float32), -6.0, 6.0)
    return values.astype(jnp.bfloat16)


def draw_frame_qkv(key, part):
    key = jax.random.fold_in(key, 12)
    table = normal_table(key, 6.0)
    return table.reshape(D, 3 * D).astype(jnp.bfloat16)


def draw_time_qkv(key, part):
    key = jax.random.fold_in(key, 13)
    table = normal_table(key, 6.0)
    return jnp.transpose(table, (1, 2, 3, 0)).reshape(3 * D, D).astype(jnp.bfloat16)


def shard_levels(own_key, dims, shards, low, high):
    loudness, own = 1.0, jax.random.fold_in(own_key, 6)
    for dim, parts in shards:
        steps = jnp.exp(jax.random.uniform(jax.random.fold_in(own, dim), (parts,), jnp.float32, low / len(shards), high / len(shards)))
        loudness = loudness * jnp.repeat(steps, dims[dim] // parts).reshape([-1 if axis == dim else 1 for axis in range(len(dims))])
    return loudness


def centred(key, dims, width, most, cuts=(), dtype=jnp.bfloat16):
    values = jax.random.normal(key, dims, jnp.float32) * width
    if len(cuts) > 0:
        values = shard_levels(key, dims, cuts, -0.22, 0.18) * values
    return jnp.clip(values, min=-most, max=most).astype(dtype)


def setup_inputs(seed: int = 0, part: int = 0) -> dict:
    streams_of = jax.random.split(jax.random.key(seed), 7)
    part_splits = jax.random.split(jax.random.fold_in(streams_of[6], part), 7)
    return {
        "tokens": draw_tokens(jax.random.fold_in(jax.random.fold_in(streams_of[6], part), 71), part),
        "frame_qkv": draw_frame_qkv(jax.random.fold_in(streams_of[6], 71), part),
        "frame_out": centred(streams_of[2], (D, D), (D // 4) ** -0.5, 0.375, ((0, 8),)),
        "time_qkv": draw_time_qkv(jax.random.fold_in(streams_of[6], 71), part),
        "time_out": centred(streams_of[4], (D, D), (D // 4) ** -0.5, 0.375),
        "modulation": centred(part_splits[5], (2, 3, D), 0.7, 4.0, (), jnp.float32),
    }


eps_norm = 1e-06

def modulate(tokens, offset, stretch):
    values = tokens.astype(jnp.float32)
    center = lax.optimization_barrier(jnp.mean(values, axis=-1, keepdims=True))
    spread = lax.optimization_barrier(jnp.mean(jnp.square(values - center), axis=-1, keepdims=True))
    normed = (values - center) * lax.rsqrt(spread + eps_norm)
    return (normed * (1.0 + stretch) + offset).astype(jnp.bfloat16)

def widen(array):
    return lax.optimization_barrier(array).astype(jnp.float32)

def normalized_weights(scores):
    largest = lax.optimization_barrier(jnp.max(scores, axis=-1, keepdims=True))
    raised = jnp.exp(scores - largest)
    return (raised / lax.optimization_barrier(jnp.sum(raised, axis=-1, keepdims=True))).astype(jnp.bfloat16)

def reference(tokens, frame_qkv, frame_out, time_qkv, time_out, modulation):
    flat_count = FRAMES * SPATIAL
    group_width = D // N_SPACE
    out_table = frame_out.astype(jnp.float32).reshape(N_SPACE, group_width, D)
    first_input = modulate(tokens, modulation[0, 0], modulation[0, 1])
    triples = jnp.dot(first_input.reshape(flat_count, D), frame_qkv, preferred_element_type=jnp.float32)
    triples = triples.astype(jnp.bfloat16).reshape(FRAMES, SPATIAL, HEADS, 3, HD)

    def frame_step(frame_in):
        queries = widen(frame_in[:, :, 0])
        key_part = widen(frame_in[:, :, 1])
        value_part = widen(frame_in[:, :, 2])
        scores = jnp.einsum('shd,thd->hst', queries, key_part) * HD ** (-0.5)
        weights = widen(normalized_weights(scores))
        attended = jnp.einsum('hst,thd->shd', weights, value_part).astype(jnp.bfloat16)
        grouped = widen(attended.reshape(SPATIAL, N_SPACE, group_width))
        partial_terms = jnp.einsum('sgc,gcd->gsd', grouped, out_table)
        return lax.optimization_barrier(jnp.sum(widen(partial_terms.astype(jnp.bfloat16)), axis=0))
    frame_branch = lax.map(frame_step, triples)
    middle = (tokens.astype(jnp.float32) + modulation[0, 2] * frame_branch).astype(jnp.bfloat16)
    second_input = modulate(middle, modulation[1, 0], modulation[1, 1])
    triples = jnp.dot(second_input.reshape(flat_count, D), time_qkv.T, preferred_element_type=jnp.float32)
    triples = triples.astype(jnp.bfloat16).reshape(FRAMES, SPATIAL, HEADS, 3, HD)
    queries = widen(triples[:, :, :, 0])
    key_part = widen(triples[:, :, :, 1])
    value_part = widen(triples[:, :, :, 2])
    scores = jnp.einsum('tshe,ushe->shtu', queries, key_part) * HD ** (-0.5)
    weights = widen(normalized_weights(scores))
    attended = jnp.einsum('shtu,ushe->tshe', weights, value_part).astype(jnp.bfloat16)
    time_branch = jnp.dot(attended.reshape(flat_count, D), time_out, preferred_element_type=jnp.float32)
    time_branch = time_branch.reshape(FRAMES, SPATIAL, D)
    return (widen(middle) + modulation[1, 2] * time_branch).astype(jnp.bfloat16)
```

```python
import math

import jax
import jax.numpy as jnp
from jax import lax
from jax.experimental import pallas as pl
from jax.experimental.pallas import tpu as pltpu
from jax.sharding import Mesh
from jax.sharding import PartitionSpec as P

HD = 72
HP = 80
LANES = 128
EPS = 1e-06
EXP2_SCALE = HD ** (-0.5) * math.log2(math.e)
NT = (((1,), (1,)), ((), ()))
TN = (((0,), (0,)), ((), ()))
VMEM_BYTES = 56 * 1024 * 1024


def params(mib=48):
    return pltpu.CompilerParams(vmem_limit_bytes=mib * 1024 * 1024)


def whole():
    return pl.BlockSpec(memory_space=pltpu.VMEM)


def modulated(values, offset, stretch):
    center = jnp.mean(values, axis=-1, keepdims=True)
    values = values - center
    spread = jnp.mean(values * values, axis=-1, keepdims=True)
    return (values * lax.rsqrt(spread + EPS) * (1.0 + stretch) + offset).astype(jnp.bfloat16)


def first_norm_kernel(tokens_ref, modulation_ref, out_ref):
    out_ref[...] = modulated(
        tokens_ref[...].astype(jnp.float32), modulation_ref[0, 0:1], modulation_ref[0, 1:2]
    )


def frame_kernel(*refs):
    pieces, (wqk_ref, wvt_ref, out_ref, qk_ref, vt_ref) = refs[:-5], refs[-5:]
    row = 0
    for piece in pieces:
        count = piece.shape[0]
        step = min(count, 256)
        for start in range(0, count, step):
            part = piece[start : start + step]
            qk_ref[row : row + step] = jnp.dot(
                part, wqk_ref[...], preferred_element_type=jnp.float32
            ).astype(jnp.bfloat16)
            values = lax.dot_general(wvt_ref[...], part, NT, preferred_element_type=jnp.float32)
            index = lax.broadcasted_iota(jnp.int32, values.shape, 0)
            ones = (index == HD) | (index == HP + HD)
            vt_ref[:, row : row + step] = jnp.where(ones, 1.0, values).astype(jnp.bfloat16)
            row += step
    block = 256
    for start in range(0, row, block):
        outs = []
        for head in range(2):
            column = 2 * LANES * head
            queries = qk_ref[start : start + block, column : column + LANES]
            keys = qk_ref[:, column + LANES : column + 2 * LANES]
            scores = lax.dot_general(keys, queries, NT, preferred_element_type=jnp.float32)
            largest = jnp.max(scores, axis=0, keepdims=True)
            raised = jnp.exp2((scores - largest) * EXP2_SCALE).astype(jnp.bfloat16)
            mixed = jnp.dot(
                vt_ref[HP * head : HP * head + HP], raised, preferred_element_type=jnp.float32
            )
            outs.append(mixed[:HD] / mixed[HD : HD + 1])
        both = jnp.concatenate(outs, axis=0).astype(jnp.bfloat16)
        for part in range(block // LANES):
            out_ref[start // LANES + part] = both[:, part * LANES : (part + 1) * LANES]


def middle_kernel(mixed_ref, table_ref, tokens_ref, modulation_ref, out_ref):
    mixed = mixed_ref[...].reshape(-1, LANES)
    branch = lax.dot_general(mixed, table_ref[...], TN, preferred_element_type=jnp.float32)
    out_ref[...] = (
        tokens_ref[...].astype(jnp.float32) + modulation_ref[0, 2:3] * branch
    ).astype(jnp.bfloat16)


def time_kernel(positions, middle_ref, table_ref, out_table_ref, modulation_ref, out_ref, input_ref, mixed_ref):
    step = pl.program_id(0)

    @pl.when(step == 0)
    def _():
        input_ref[...] = modulated(
            middle_ref[...].astype(jnp.float32), modulation_ref[1, 0:1], modulation_ref[1, 1:2]
        )

    rows = input_ref.shape[0]
    one = lax.broadcasted_iota(jnp.int32, (rows, rows), 0) % positions
    two = lax.broadcasted_iota(jnp.int32, (rows, rows), 1) % positions
    same = one == two
    heads = table_ref.shape[0]
    outs = []
    for head in range(heads):
        table = table_ref[head].reshape(-1, table_ref.shape[-1])
        triple = lax.dot_general(
            table, input_ref[...], NT, preferred_element_type=jnp.float32
        ).astype(jnp.bfloat16)
        queries, keys, values = triple[:HP], triple[HP : 2 * HP], triple[2 * HP : 3 * HP]
        scores = lax.dot_general(keys, queries, TN, preferred_element_type=jnp.float32)
        scores = jnp.where(same, scores, -1e30)
        largest = jnp.max(scores, axis=0, keepdims=True)
        raised = jnp.exp2((scores - largest) * EXP2_SCALE)
        total = jnp.sum(raised, axis=0, keepdims=True)
        mixed = jnp.dot(values, raised.astype(jnp.bfloat16), preferred_element_type=jnp.float32)
        outs.append(mixed[:HD] / total)
    mixed_ref[step] = jnp.concatenate(outs, axis=0).astype(jnp.bfloat16)

    @pl.when(step == pl.num_programs(0) - 1)
    def _():
        mixed = mixed_ref[...].reshape(-1, rows)
        branch = lax.dot_general(mixed, out_table_ref[...], TN, preferred_element_type=jnp.float32)
        out_ref[...] = (
            middle_ref[...].astype(jnp.float32) + modulation_ref[1, 2:3] * branch
        ).astype(jnp.bfloat16)


def rotation(count, by):
    return [(index, (index + by) % count) for index in range(count)]


SWAP = [(0, 1), (1, 0)]


def shards(tokens, frame_qkv, frame_out, time_qkv, time_out, modulation):
    tokens = tokens[0]
    rows, width = tokens.shape
    zh = lax.axis_index("zh")

    part = jnp.pad(time_qkv.reshape(3, HD, width), ((0, 0), (0, HP - HD), (0, 0)))
    part = jnp.pad(part.reshape(3 * HP, width), ((0, 256 - 3 * HP), (0, 0)))
    index = lax.axis_index("y") * 2 + lax.axis_index("c")
    part = lax.dynamic_slice_in_dim(part, index * 32, 32, 0)
    time_table = lax.all_gather(part, ("x", "zl", "y", "c"), axis=0)
    time_table = time_table.reshape(16, 8, 32, width)

    index = jnp.minimum(lax.axis_index("x") * 4 + lax.axis_index("y"), 8)
    part = lax.dynamic_slice_in_dim(frame_out, index * 16, 16, 0)
    out_table = lax.all_gather(part, ("zh", "c", "x", "y"), axis=0)
    out_table = out_table.reshape(8, 16, 16, width)[:, :9].reshape(width, width)

    heads = frame_qkv.reshape(width, 2, 3, HD)
    wqk = jnp.pad(heads[:, :, :2], ((0, 0), (0, 0), (0, 0), (0, LANES - HD))).reshape(width, 4 * LANES)
    wvt = jnp.pad(jnp.transpose(heads[:, :, 2], (1, 2, 0)), ((0, 0), (0, HP - HD), (0, 0)))
    wvt = wvt.reshape(2 * HP, width)

    first_input = pl.pallas_call(
        first_norm_kernel,
        out_shape=jax.ShapeDtypeStruct((rows, width), jnp.bfloat16),
        in_specs=[whole(), whole()],
        out_specs=whole(),
        compiler_params=params(),
        name="first_norm",
    )(tokens, modulation)

    gathered = lax.all_gather(first_input, ("zh", "c"), axis=0, tiled=True)

    total = gathered.shape[0]
    mixed = pl.pallas_call(
        frame_kernel,
        out_shape=jax.ShapeDtypeStruct((total // LANES, 2 * HD, LANES), jnp.bfloat16),
        in_specs=[whole()] * 3,
        out_specs=whole(),
        scratch_shapes=[
            pltpu.VMEM((total, 4 * LANES), jnp.bfloat16),
            pltpu.VMEM((2 * HP, total), jnp.bfloat16),
        ],
        compiler_params=params(),
        name="frame_attention",
    )(gathered, wqk, wvt)

    mixed = lax.all_to_all(mixed, ("zh", "c"), 0, 0, tiled=True)
    middle = pl.pallas_call(
        middle_kernel,
        out_shape=jax.ShapeDtypeStruct((rows, width), jnp.bfloat16),
        in_specs=[whole()] * 4,
        out_specs=whole(),
        compiler_params=params(),
        name="middle",
    )(mixed, out_table, tokens, modulation)

    middle = lax.all_to_all(middle, ("x", "zl"), 0, 0, tiled=True)

    positions = rows // 16
    group = 2
    steps = 16 // group
    out = pl.pallas_call(
        lambda *refs: time_kernel(positions, *refs),
        grid=(steps,),
        out_shape=jax.ShapeDtypeStruct((rows, width), jnp.bfloat16),
        in_specs=[
            whole(),
            pl.BlockSpec((group, 8, 32, width), lambda i: (i, 0, 0, 0)),
            whole(),
            whole(),
        ],
        out_specs=whole(),
        scratch_shapes=[
            pltpu.VMEM((rows, width), jnp.bfloat16),
            pltpu.VMEM((steps, group * HD, rows), jnp.bfloat16),
        ],
        compiler_params=params(),
        name="time_block",
    )(middle, time_table, time_out, modulation)
    out = lax.all_to_all(out, ("x", "zl"), 0, 0, tiled=True)
    return out[None]


def solution(mesh):
    fine = Mesh(mesh.devices.reshape(4, 4, 4, 4, 2), ("y", "x", "zl", "zh", "c"))
    frames, space = ("y", "x", "zl"), ("zh", "c")
    placed = (
        P(frames, space, None),
        P(None, space),
        P(space, None),
        P(("x", "zl"), None),
        P(),
        P("y", None, None),
    )
    return jax.shard_map(
        shards,
        mesh=fine,
        in_specs=placed,
        out_specs=P(frames, space, None),
        check_vma=False,
    )
```

```python
import functools
import math

import jax
import jax.numpy as jnp
from jax import lax
from jax.experimental import pallas as pl
from jax.experimental.pallas import tpu as pltpu
from jax.sharding import Mesh
from jax.sharding import PartitionSpec as P

HD = 72
HP = 80
LANES = 128
EPS = 1e-06
EXP2_SCALE = HD ** (-0.5) * math.log2(math.e)
NT = (((1,), (1,)), ((), ()))
TN = (((0,), (0,)), ((), ()))


def params(mib=48):
    return pltpu.CompilerParams(vmem_limit_bytes=mib * 1024 * 1024)


def whole():
    return pl.BlockSpec(memory_space=pltpu.VMEM)


def modulated(values, offset, stretch):
    center = jnp.mean(values, axis=-1, keepdims=True)
    values = values - center
    spread = jnp.mean(values * values, axis=-1, keepdims=True)
    return (values * lax.rsqrt(spread + EPS) * (1.0 + stretch) + offset).astype(jnp.bfloat16)


def triples_of(rows, modulation_ref, wqk_ref, wvt_ref):
    normed = modulated(rows, modulation_ref[0, 0:1], modulation_ref[0, 1:2])
    qk = jnp.dot(normed, wqk_ref[...], preferred_element_type=jnp.float32).astype(jnp.bfloat16)
    values = lax.dot_general(wvt_ref[...], normed, NT, preferred_element_type=jnp.float32)
    index = lax.broadcasted_iota(jnp.int32, values.shape, 0)
    ones = (index == HD) | (index == HP + HD)
    return qk, jnp.where(ones, 1.0, values).astype(jnp.bfloat16)


def early_kernel(*refs):
    pieces, (modulation_ref, wqk_ref, wvt_ref, qk_ref, vt_ref) = refs[:-5], refs[-5:]
    for index in range(0, len(pieces), 2):
        rows = jnp.concatenate([pieces[index][...], pieces[index + 1][...]], axis=0)
        qk, vt = triples_of(rows.astype(jnp.float32), modulation_ref, wqk_ref, wvt_ref)
        start = LANES * index
        qk_ref[start : start + 2 * LANES] = qk
        vt_ref[:, start : start + 2 * LANES] = vt


def frame_kernel(
    place_ref, one_ref, two_ref, three_ref, four_ref, qk_ref, vt_ref, modulation_ref, wqk_ref, wvt_ref,
    out_ref, qk_late_ref, vt_late_ref,
):
    rows = jnp.concatenate([one_ref[...], two_ref[...], three_ref[...], four_ref[...]], axis=0)
    qk_late_ref[...], vt_late_ref[...] = triples_of(
        rows.astype(jnp.float32), modulation_ref, wqk_ref, wvt_ref
    )
    parts = ((qk_ref, vt_ref), (qk_late_ref, vt_late_ref))
    block = 2 * LANES
    number = 0
    for qk_part, _ in parts:
        for start in range(0, qk_part.shape[0], block):
            outs = []
            for head in range(2):
                column = 2 * LANES * head
                queries = qk_part[start : start + block, column : column + LANES]
                scores = [
                    lax.dot_general(
                        qk[:, column + LANES : column + 2 * LANES], queries, NT,
                        preferred_element_type=jnp.float32,
                    )
                    for qk, _ in parts
                ]
                largest = jnp.maximum(*[jnp.max(part, axis=0, keepdims=True) for part in scores])
                mixed = sum(
                    jnp.dot(
                        vt[HP * head : HP * head + HP],
                        jnp.exp2((part - largest) * EXP2_SCALE).astype(jnp.bfloat16),
                        preferred_element_type=jnp.float32,
                    )
                    for part, (_, vt) in zip(scores, parts)
                )
                outs.append(mixed[:HD] / mixed[HD : HD + 1])
            both = jnp.concatenate(outs, axis=0).astype(jnp.bfloat16)
            for part in range(2):
                out_ref[place_ref[number]] = both[:, part * LANES : (part + 1) * LANES]
                number += 1


def middle_kernel(place_ref, mixed_ref, tables_ref, tokens_ref, modulation_ref, out_ref, table_ref, sem):
    copy = pltpu.make_async_copy(tables_ref.at[pl.ds(0, 9), :, pl.ds(LANES, 64), :], table_ref, sem)
    copy.start()
    zh = place_ref[8]
    slots = [mixed_ref[((zh + 4 - slot) % 4) * 2 + core] for core in range(2) for slot in range(4)]
    mixed = jnp.concatenate(
        [slot[16 * number : 16 * number + 16] for number in range(9) for slot in slots], axis=0
    )
    copy.wait()
    table = table_ref[...].reshape(-1, table_ref.shape[-1])
    branch = lax.dot_general(mixed, table, TN, preferred_element_type=jnp.float32)
    out_ref[...] = (
        tokens_ref[...].astype(jnp.float32) + modulation_ref[0, 2:3] * branch
    ).astype(jnp.bfloat16)


def time_kernel(
    positions, place_ref, middle_ref, tables_ref, out_table_ref, modulation_ref, out_ref,
    input_ref, mixed_ref, table_ref, sem,
):
    step = pl.program_id(0)
    copy = pltpu.make_async_copy(out_table_ref, table_ref, sem)

    @pl.when(step == 0)
    def _():
        copy.start()
        input_ref[...] = modulated(
            middle_ref[...].astype(jnp.float32), modulation_ref[1, 0:1], modulation_ref[1, 1:2]
        )

    rows, width = input_ref.shape
    zl = place_ref[9]
    one = lax.broadcasted_iota(jnp.int32, (rows, rows), 0) % positions
    two = lax.broadcasted_iota(jnp.int32, (rows, rows), 1) % positions
    same = one == two
    triples = []
    for slot in range(4):
        table = tables_ref[0, 0:7, 32 * slot : 32 * slot + 32].reshape(7 * 32, width)
        triples.append(lax.dot_general(table, input_ref[...], NT, preferred_element_type=jnp.float32))
    scores = []
    for triple in triples:
        queries = triple[:HD].astype(jnp.bfloat16)
        keys = triple[HD : 2 * HD].astype(jnp.bfloat16)
        part = lax.dot_general(keys, queries, TN, preferred_element_type=jnp.float32)
        scores.append(jnp.where(same, part, -1e30))
    raised = [
        jnp.exp2((part - jnp.max(part, axis=0, keepdims=True)) * EXP2_SCALE) for part in scores
    ]
    for slot in range(4):
        values = jnp.concatenate([triples[slot][2 * HD : 192], triples[slot][200:]], axis=0)
        total = jnp.sum(raised[slot], axis=0, keepdims=True)
        mixed = jnp.dot(
            values.astype(jnp.bfloat16), raised[slot].astype(jnp.bfloat16),
            preferred_element_type=jnp.float32,
        )
        mixed_ref[step * 4 + (zl + 4 - slot) % 4] = mixed / total

    @pl.when(step == pl.num_programs(0) - 1)
    def _():
        copy.wait()
        mixed = mixed_ref[...].reshape(-1, rows).astype(jnp.bfloat16)
        branch = lax.dot_general(mixed, table_ref[...], TN, preferred_element_type=jnp.float32)
        out_ref[...] = (
            middle_ref[...].astype(jnp.float32) + modulation_ref[1, 2:3] * branch
        ).astype(jnp.bfloat16)


def rotation(count, by):
    return [(index, (index + by) % count) for index in range(count)]


SWAP = [(0, 1), (1, 0)]


def shards(tokens, frame_qkv, frame_out, time_qkv, time_out, modulation):
    tokens = tokens[0]
    rows, width = tokens.shape
    half = rows // 2
    zh, zl, core = lax.axis_index("zh"), lax.axis_index("zl"), lax.axis_index("c")

    def along(array, axis, by):
        return lax.ppermute(array, axis, rotation(4, by))

    def swapped(array):
        return lax.ppermute(array, "c", SWAP)

    before, after = along(tokens, "zh", 1), along(tokens, "zh", 3)
    beside = swapped(tokens)
    far_top, far_bottom = along(before[:half], "zh", 1), along(after[half:], "zh", 3)
    early = [tokens, beside, before, swapped(before), after, swapped(after)]
    late = [far_top, far_bottom, swapped(far_top), swapped(far_bottom)]
    spots = [zh, (zh + 3) % 4, (zh + 1) % 4, (zh + 2) % 4]
    place = jnp.stack(
        [spot * 2 + side for spot in spots for side in (core, 1 - core)] + [zh, zl]
    ).astype(jnp.int32)

    index = lax.axis_index("y") * 2 + core
    time_part = lax.dynamic_slice_in_dim(time_qkv, jnp.minimum(index * 32, 216 - 32), 32, 0)
    index = lax.axis_index("x") * 4 + lax.axis_index("y")
    out_part = lax.dynamic_slice_in_dim(frame_out, jnp.minimum(index, 8) * 16, 16, 0)
    parts = [time_part] + [along(time_part, "zl", by) for by in (1, 2, 3)]
    parts += [out_part] + [along(out_part, "zh", by) for by in (1, 2, 3)]
    tables = lax.all_gather(jnp.concatenate(parts, axis=0), ("x", "y", "c"), axis=0)
    tables = tables.reshape(4, 8, 192, width)

    heads = frame_qkv.reshape(width, 2, 3, HD)
    wqk = jnp.pad(heads[:, :, :2], ((0, 0), (0, 0), (0, 0), (0, LANES - HD))).reshape(width, 4 * LANES)
    wvt = jnp.pad(jnp.transpose(heads[:, :, 2], (1, 2, 0)), ((0, 0), (0, HP - HD), (0, 0)))
    wvt = wvt.reshape(2 * HP, width)

    soon = rows * len(early)
    qk, vt = pl.pallas_call(
        early_kernel,
        out_shape=(
            jax.ShapeDtypeStruct((soon, 4 * LANES), jnp.bfloat16),
            jax.ShapeDtypeStruct((2 * HP, soon), jnp.bfloat16),
        ),
        in_specs=[whole()] * (len(early) + 3),
        out_specs=(whole(), whole()),
        compiler_params=params(),
        cost_estimate=pl.CostEstimate(flops=2 * 10**9, bytes_accessed=5 * 10**6, transcendentals=0),
        name="early_triples",
    )(*early, modulation, wqk, wvt)

    rest = 2 * rows
    mixed = pl.pallas_call(
        frame_kernel,
        out_shape=jax.ShapeDtypeStruct(((soon + rest) // LANES, 2 * HD, LANES), jnp.bfloat16),
        in_specs=[pl.BlockSpec(memory_space=pltpu.SMEM)] + [whole()] * 9,
        out_specs=whole(),
        scratch_shapes=[
            pltpu.VMEM((rest, 4 * LANES), jnp.bfloat16),
            pltpu.VMEM((2 * HP, rest), jnp.bfloat16),
        ],
        compiler_params=params(),
        name="frame_attention",
    )(place, *late, qk, vt, modulation, wqk, wvt)

    mixed = lax.all_to_all(mixed, ("zh", "c"), 0, 0, tiled=True)
    middle = pl.pallas_call(
        middle_kernel,
        out_shape=jax.ShapeDtypeStruct((rows, width), jnp.bfloat16),
        in_specs=[
            pl.BlockSpec(memory_space=pltpu.SMEM), whole(), pl.BlockSpec(memory_space=pl.ANY), whole(), whole()
        ],
        out_specs=whole(),
        scratch_shapes=[pltpu.VMEM((9, 2, 64, width), jnp.bfloat16), pltpu.SemaphoreType.DMA],
        compiler_params=params(),
        name="middle",
    )(place, mixed, tables.reshape(16, 2, 192, width), tokens, modulation)

    middle = lax.all_to_all(middle, ("x", "zl"), 0, 0, tiled=True)

    out = pl.pallas_call(
        functools.partial(time_kernel, rows // 16),
        grid=(4,),
        out_shape=jax.ShapeDtypeStruct((rows, width), jnp.bfloat16),
        in_specs=[
            pl.BlockSpec(memory_space=pltpu.SMEM),
            whole(),
            pl.BlockSpec((1, 8, LANES, width), lambda i: (i, 0, 0, 0)),
            pl.BlockSpec(memory_space=pl.ANY),
            whole(),
        ],
        out_specs=whole(),
        scratch_shapes=[
            pltpu.VMEM((rows, width), jnp.bfloat16),
            pltpu.VMEM((16, HD, rows), jnp.float32),
            pltpu.VMEM((width, width), jnp.bfloat16),
            pltpu.SemaphoreType.DMA,
        ],
        compiler_params=params(),
        name="time_block",
    )(place, middle, tables, time_out, modulation)
    out = lax.all_to_all(out, ("x", "zl"), 0, 0, tiled=True)
    return out[None]


def solution(mesh):
    fine = Mesh(mesh.devices.reshape(4, 4, 4, 4, 2), ("y", "x", "zl", "zh", "c"))
    frames, space = ("y", "x", "zl"), ("zh", "c")
    placed = (
        P(frames, space, None),
        P(None, space),
        P(space, None),
        P(("x", "zl"), None),
        P(),
        P("y", None, None),
    )
    return jax.shard_map(
        shards,
        mesh=fine,
        in_specs=placed,
        out_specs=P(frames, space, None),
        check_vma=False,
    )
```

```python
import functools
import math

import jax
import jax.numpy as jnp
from jax import lax
from jax.experimental import pallas as pl
from jax.experimental.pallas import tpu as pltpu
from jax.sharding import Mesh
from jax.sharding import PartitionSpec as P

HD = 72
HP = 80
LANES = 128
EPS = 1e-06
EXP2_SCALE = HD ** (-0.5) * math.log2(math.e)
NT = (((1,), (1,)), ((), ()))
TN = (((0,), (0,)), ((), ()))


def params(mib=48):
    return pltpu.CompilerParams(vmem_limit_bytes=mib * 1024 * 1024)


def whole():
    return pl.BlockSpec(memory_space=pltpu.VMEM)


def modulated(values, offset, stretch):
    center = jnp.mean(values, axis=-1, keepdims=True)
    values = values - center
    spread = jnp.mean(values * values, axis=-1, keepdims=True)
    return (values * lax.rsqrt(spread + EPS) * (1.0 + stretch) + offset).astype(jnp.bfloat16)


def triples_of(rows, modulation_ref, wqk_ref, wvt_ref):
    normed = modulated(rows, modulation_ref[0, 0:1], modulation_ref[0, 1:2])
    qk = jnp.dot(normed, wqk_ref[...], preferred_element_type=jnp.float32).astype(jnp.bfloat16)
    values = lax.dot_general(wvt_ref[...], normed, NT, preferred_element_type=jnp.float32)
    index = lax.broadcasted_iota(jnp.int32, values.shape, 0)
    ones = (index == HD) | (index == HP + HD)
    return qk, jnp.where(ones, 1.0, values).astype(jnp.bfloat16)


def early_kernel(own_ref, beside_ref, near_ref, swapped_ref, modulation_ref, wqk_ref, wvt_ref, qk_ref, vt_ref):
    for index, pair in enumerate(((own_ref, beside_ref), (near_ref, swapped_ref))):
        rows = jnp.concatenate([pair[0][...], pair[1][...]], axis=0)
        qk, vt = triples_of(rows.astype(jnp.float32), modulation_ref, wqk_ref, wvt_ref)
        start = 2 * LANES * index
        qk_ref[start : start + 2 * LANES] = qk
        vt_ref[:, start : start + 2 * LANES] = vt


def frame_kernel(
    place_ref, late_ref, swapped_ref, qk_ref, vt_ref, modulation_ref, wqk_ref, wvt_ref,
    out_ref, qk_late_ref, vt_late_ref,
):
    for index, rows_ref in enumerate((late_ref, swapped_ref)):
        start = 2 * LANES * index
        qk, vt = triples_of(rows_ref[...].astype(jnp.float32), modulation_ref, wqk_ref, wvt_ref)
        qk_late_ref[start : start + 2 * LANES] = qk
        vt_late_ref[:, start : start + 2 * LANES] = vt
    parts = ((qk_ref, vt_ref), (qk_late_ref, vt_late_ref))
    blocks = (
        ((qk_ref, 0), (qk_ref, 64), (qk_ref, 128), (qk_ref, 192)),
        ((qk_ref, 256), (qk_late_ref, 128), (qk_ref, 384), (qk_late_ref, 384)),
        ((qk_late_ref, 192), (qk_ref, 320), (qk_late_ref, 448), (qk_ref, 448)),
        ((qk_late_ref, 0), (qk_late_ref, 64), (qk_late_ref, 256), (qk_late_ref, 320)),
    )
    for number, block in enumerate(blocks):
        outs = []
        for head in range(2):
            column = 2 * LANES * head
            queries = jnp.concatenate(
                [ref[start : start + 64, column : column + LANES] for ref, start in block], axis=0
            )
            scores = [
                lax.dot_general(
                    qk[:, column + LANES : column + 2 * LANES], queries, NT,
                    preferred_element_type=jnp.float32,
                )
                for qk, _ in parts
            ]
            largest = jnp.maximum(*[jnp.max(part, axis=0, keepdims=True) for part in scores])
            mixed = sum(
                jnp.dot(
                    vt[HP * head : HP * head + HP],
                    jnp.exp2((part - largest) * EXP2_SCALE).astype(jnp.bfloat16),
                    preferred_element_type=jnp.float32,
                )
                for part, (_, vt) in zip(scores, parts)
            )
            outs.append(mixed[:HD] / mixed[HD : HD + 1])
        both = jnp.concatenate(outs, axis=0).astype(jnp.bfloat16)
        for part in range(2):
            out_ref[place_ref[2 * number + part]] = both[:, part * LANES : (part + 1) * LANES]


def join_kernel(mixed_ref, tokens_ref, out_ref):
    width = tokens_ref.shape[1]
    mixed = mixed_ref[...].reshape(-1, LANES).astype(jnp.float32)
    out_ref[:, :width] = mixed.T.astype(jnp.bfloat16)
    out_ref[:, width:] = tokens_ref[...]


def time_kernel(
    positions, place_ref, joined_ref, tables_ref, all_ref, out_table_ref, modulation_ref, out_ref,
    middle_ref, input_ref, mixed_ref, frame_table_ref, time_table_ref, frame_sem, time_sem,
):
    step = pl.program_id(0)
    rows, width = input_ref.shape
    zh, zl = place_ref[8], place_ref[9]
    time_copy = pltpu.make_async_copy(out_table_ref, time_table_ref, time_sem)

    @pl.when(step == 0)
    def _():
        frame_copies = [
            pltpu.make_async_copy(
                all_ref.at[pl.ds(0, 9), core, pl.ds(LANES + 16 * slot, 16), :],
                frame_table_ref.at[2 * ((zh + 4 - slot) % 4) + core],
                frame_sem.at[2 * slot + core],
            )
            for slot in range(4)
            for core in range(2)
        ]
        for copy in frame_copies:
            copy.start()
        time_copy.start()
        for copy in frame_copies:
            copy.wait()
        table = frame_table_ref[...].reshape(width, width)
        branch = jnp.dot(joined_ref[:, :width], table, preferred_element_type=jnp.float32)
        middle = joined_ref[:, width:].astype(jnp.float32) + modulation_ref[0, 2:3] * branch
        middle = middle.astype(jnp.bfloat16)
        middle_ref[...] = middle
        input_ref[...] = modulated(
            middle.astype(jnp.float32), modulation_ref[1, 0:1], modulation_ref[1, 1:2]
        )

    @pl.when(step > 0)
    def _():
        one = lax.broadcasted_iota(jnp.int32, (rows, rows), 0) % positions
        two = lax.broadcasted_iota(jnp.int32, (rows, rows), 1) % positions
        same = one == two
        triples = []
        for head in range(4):
            table = tables_ref[0, 0:7, 32 * head : 32 * head + 32].reshape(7 * 32, width)
            triples.append(
                lax.dot_general(table, input_ref[...], NT, preferred_element_type=jnp.float32)
            )
        scores = []
        for triple in triples:
            queries = triple[:HD].astype(jnp.bfloat16)
            keys = triple[HD : 2 * HD].astype(jnp.bfloat16)
            part = lax.dot_general(keys, queries, TN, preferred_element_type=jnp.float32)
            scores.append(jnp.where(same, part, -1e30))
        raised = [
            jnp.exp2((part - jnp.max(part, axis=0, keepdims=True)) * EXP2_SCALE) for part in scores
        ]
        for head in range(4):
            values = jnp.concatenate([triples[head][2 * HD : 192], triples[head][200:]], axis=0)
            total = jnp.sum(raised[head], axis=0, keepdims=True)
            mixed = jnp.dot(
                values.astype(jnp.bfloat16), raised[head].astype(jnp.bfloat16),
                preferred_element_type=jnp.float32,
            )
            mixed_ref[(step - 1) * 4 + (zl + 4 - head) % 4] = mixed / total

    @pl.when(step == pl.num_programs(0) - 1)
    def _():
        time_copy.wait()
        mixed = mixed_ref[...].reshape(-1, rows).astype(jnp.bfloat16)
        branch = lax.dot_general(mixed, time_table_ref[...], TN, preferred_element_type=jnp.float32)
        out_ref[...] = (
            middle_ref[...].astype(jnp.float32) + modulation_ref[1, 2:3] * branch
        ).astype(jnp.bfloat16)


def rotation(count, by):
    return [(index, (index + by) % count) for index in range(count)]


SWAP = [(0, 1), (1, 0)]


def shards(tokens, frame_qkv, frame_out, time_qkv, time_out, modulation):
    tokens = tokens[0]
    rows, width = tokens.shape
    half = rows // 2
    zh, zl, core = lax.axis_index("zh"), lax.axis_index("zl"), lax.axis_index("c")

    def along(array, axis, by):
        return lax.ppermute(array, axis, rotation(4, by))

    def swapped(array):
        return lax.ppermute(array, "c", SWAP)

    index = lax.axis_index("y") * 2 + core
    time_part = lax.dynamic_slice_in_dim(time_qkv, jnp.minimum(index * 32, 216 - 32), 32, 0)
    index = lax.axis_index("x") * 4 + lax.axis_index("y")
    out_part = lax.dynamic_slice_in_dim(frame_out, jnp.minimum(index, 8) * 16, 16, 0)

    beside = swapped(tokens)
    below = along(jnp.concatenate([tokens[:half], out_part], axis=0), "zh", 1)
    above = along(jnp.concatenate([tokens[half:], out_part], axis=0), "zh", 3)
    near = jnp.concatenate([below[:half], above[:half]], axis=0)
    far_top, far_bottom = along(below[:half], "zh", 1), along(above[:half], "zh", 3)
    below_bottom, above_top = along(tokens[half:], "zh", 1), along(tokens[:half], "zh", 3)
    late = jnp.concatenate([far_top, far_bottom, below_bottom, above_top], axis=0)

    parts = [time_part] + [along(time_part, "zl", by) for by in (1, 2, 3)]
    parts += [out_part, below[half:], along(out_part, "zh", 2), above[half:]]
    tables = lax.all_gather(jnp.concatenate(parts, axis=0), ("x", "y", "c"), axis=0)
    tables = tables.reshape(4, 8, 192, width)

    spots = [zh, (zh + 3) % 4, (zh + 1) % 4, (zh + 2) % 4]
    place = [spot * 2 + side for spot in spots for side in (core, 1 - core)]
    place = jnp.stack(place + [zh, zl]).astype(jnp.int32)

    heads = frame_qkv.reshape(width, 2, 3, HD)
    wqk = jnp.pad(heads[:, :, :2], ((0, 0), (0, 0), (0, 0), (0, LANES - HD))).reshape(width, 4 * LANES)
    wvt = jnp.pad(jnp.transpose(heads[:, :, 2], (1, 2, 0)), ((0, 0), (0, HP - HD), (0, 0)))
    wvt = wvt.reshape(2 * HP, width)

    count = 4 * rows
    shapes = (
        jax.ShapeDtypeStruct((count, 4 * LANES), jnp.bfloat16),
        jax.ShapeDtypeStruct((2 * HP, count), jnp.bfloat16),
    )
    qk, vt = pl.pallas_call(
        early_kernel,
        out_shape=shapes,
        in_specs=[whole()] * 7,
        out_specs=(whole(), whole()),
        compiler_params=params(),
        cost_estimate=pl.CostEstimate(flops=10**9, bytes_accessed=5 * 10**6, transcendentals=0),
        name="early_triples",
    )(tokens, beside, near, swapped(near), modulation, wqk, wvt)

    mixed = pl.pallas_call(
        frame_kernel,
        out_shape=jax.ShapeDtypeStruct((2 * count // LANES, 2 * HD, LANES), jnp.bfloat16),
        in_specs=[pl.BlockSpec(memory_space=pltpu.SMEM)] + [whole()] * 7,
        out_specs=whole(),
        scratch_shapes=[pltpu.VMEM(shape.shape, shape.dtype) for shape in shapes],
        compiler_params=params(),
        name="frame_attention",
    )(place, late, swapped(late), qk, vt, modulation, wqk, wvt)

    mixed = lax.all_to_all(mixed, ("zh", "c"), 0, 0, tiled=True)
    joined = pl.pallas_call(
        join_kernel,
        out_shape=jax.ShapeDtypeStruct((rows, 2 * width), jnp.bfloat16),
        in_specs=[whole(), whole()],
        out_specs=whole(),
        compiler_params=params(),
        name="join",
    )(mixed, tokens)
    joined = lax.all_to_all(joined, ("x", "zl"), 0, 0, tiled=True)

    out = pl.pallas_call(
        functools.partial(time_kernel, rows // 16),
        grid=(5,),
        out_shape=jax.ShapeDtypeStruct((rows, width), jnp.bfloat16),
        in_specs=[
            pl.BlockSpec(memory_space=pltpu.SMEM),
            whole(),
            pl.BlockSpec((1, 8, LANES, width), lambda i: (jnp.maximum(i - 1, 0), 0, 0, 0)),
            pl.BlockSpec(memory_space=pl.ANY),
            pl.BlockSpec(memory_space=pl.ANY),
            whole(),
        ],
        out_specs=whole(),
        scratch_shapes=[
            pltpu.VMEM((rows, width), jnp.bfloat16),
            pltpu.VMEM((rows, width), jnp.bfloat16),
            pltpu.VMEM((16, HD, rows), jnp.float32),
            pltpu.VMEM((8, 9, 16, width), jnp.bfloat16),
            pltpu.VMEM((width, width), jnp.bfloat16),
            pltpu.SemaphoreType.DMA((8,)),
            pltpu.SemaphoreType.DMA,
        ],
        compiler_params=params(),
        name="time_block",
    )(place, joined, tables, tables.reshape(16, 2, 192, width), time_out, modulation)
    out = lax.all_to_all(out, ("x", "zl"), 0, 0, tiled=True)
    return out[None]


def solution(mesh):
    fine = Mesh(mesh.devices.reshape(4, 4, 4, 4, 2), ("y", "x", "zl", "zh", "c"))
    frames, space = ("y", "x", "zl"), ("zh", "c")
    placed = (
        P(frames, space, None),
        P(None, space),
        P(space, None),
        P(("x", "zl"), None),
        P(),
        P("y", None, None),
    )
    return jax.shard_map(
        shards,
        mesh=fine,
        in_specs=placed,
        out_specs=P(frames, space, None),
        check_vma=False,
    )
```

```python
import functools
import math

import jax
import jax.numpy as jnp
from jax import lax
from jax.experimental import pallas as pl
from jax.experimental.pallas import tpu as pltpu
from jax.sharding import Mesh
from jax.sharding import PartitionSpec as P

HD = 72
HP = 80
LANES = 128
EPS = 1e-06
EXP2_SCALE = HD ** (-0.5) * math.log2(math.e)
NT = (((1,), (1,)), ((), ()))
TN = (((0,), (0,)), ((), ()))


def params(mib=48):
    return pltpu.CompilerParams(vmem_limit_bytes=mib * 1024 * 1024)


def whole():
    return pl.BlockSpec(memory_space=pltpu.VMEM)


def modulated(values, offset, stretch):
    center = jnp.mean(values, axis=-1, keepdims=True)
    values = values - center
    spread = jnp.mean(values * values, axis=-1, keepdims=True)
    return (values * lax.rsqrt(spread + EPS) * (1.0 + stretch) + offset).astype(jnp.bfloat16)


def triples_of(rows, modulation_ref, wqk_ref, wvt_ref):
    normed = modulated(rows, modulation_ref[0, 0:1], modulation_ref[0, 1:2])
    qk = jnp.dot(normed, wqk_ref[...], preferred_element_type=jnp.float32).astype(jnp.bfloat16)
    values = lax.dot_general(wvt_ref[...], normed, NT, preferred_element_type=jnp.float32)
    index = lax.broadcasted_iota(jnp.int32, values.shape, 0)
    ones = (index == HD) | (index == HP + HD)
    return qk, jnp.where(ones, 1.0, values).astype(jnp.bfloat16)


def frame_kernel(tokens_ref, modulation_ref, wqk_ref, wvt_ref, out_ref, qk_ref, vt_ref):
    count, block = tokens_ref.shape[0], 2 * LANES
    for start in range(0, count, block):
        rows = tokens_ref[start : start + block].astype(jnp.float32)
        qk, vt = triples_of(rows, modulation_ref, wqk_ref, wvt_ref)
        qk_ref[start : start + block] = qk
        vt_ref[:, start : start + block] = vt
    for start in range(0, count, block):
        outs = []
        for head in range(2):
            column = 2 * LANES * head
            queries = qk_ref[start : start + block, column : column + LANES]
            keys = qk_ref[:, column + LANES : column + 2 * LANES]
            scores = lax.dot_general(keys, queries, NT, preferred_element_type=jnp.float32)
            largest = jnp.max(scores, axis=0, keepdims=True)
            raised = jnp.exp2((scores - largest) * EXP2_SCALE).astype(jnp.bfloat16)
            mixed = jnp.dot(
                vt_ref[HP * head : HP * head + HP], raised, preferred_element_type=jnp.float32
            )
            outs.append(mixed[:HD] / mixed[HD : HD + 1])
        both = jnp.concatenate(outs, axis=0).astype(jnp.bfloat16)
        for part in range(2):
            out_ref[start // LANES + part] = both[:, part * LANES : (part + 1) * LANES]


def join_kernel(mixed_ref, tokens_ref, out_ref):
    width = tokens_ref.shape[1]
    mixed = mixed_ref[...].reshape(-1, LANES).astype(jnp.float32)
    out_ref[:, :width] = mixed.T.astype(jnp.bfloat16)
    out_ref[:, width:] = tokens_ref[...]


def time_kernel(
    positions, joined_ref, tables_ref, all_ref, out_table_ref, modulation_ref, out_ref,
    middle_ref, input_ref, mixed_ref, frame_table_ref, time_table_ref, frame_sem, time_sem,
):
    step = pl.program_id(0)
    rows, width = input_ref.shape
    time_copy = pltpu.make_async_copy(out_table_ref, time_table_ref, time_sem)

    @pl.when(step == 0)
    def _():
        frame_copies = [
            pltpu.make_async_copy(
                all_ref.at[pl.ds(0, 9), core, pl.ds(LANES + 16 * zh, 16), :],
                frame_table_ref.at[2 * zh + core],
                frame_sem.at[2 * zh + core],
            )
            for zh in range(4)
            for core in range(2)
        ]
        for copy in frame_copies:
            copy.start()
        time_copy.start()
        for copy in frame_copies:
            copy.wait()
        table = frame_table_ref[...].reshape(width, width)
        branch = jnp.dot(joined_ref[:, :width], table, preferred_element_type=jnp.float32)
        middle = joined_ref[:, width:].astype(jnp.float32) + modulation_ref[0, 2:3] * branch
        middle = middle.astype(jnp.bfloat16)
        middle_ref[...] = middle
        input_ref[...] = modulated(
            middle.astype(jnp.float32), modulation_ref[1, 0:1], modulation_ref[1, 1:2]
        )

    @pl.when(step > 0)
    def _():
        one = lax.broadcasted_iota(jnp.int32, (rows, rows), 0) % positions
        two = lax.broadcasted_iota(jnp.int32, (rows, rows), 1) % positions
        same = one == two
        triples = []
        for head in range(4):
            table = tables_ref[0, 0:7, 32 * head : 32 * head + 32].reshape(7 * 32, width)
            triples.append(
                lax.dot_general(table, input_ref[...], NT, preferred_element_type=jnp.float32)
            )
        scores = []
        for triple in triples:
            queries = triple[:HD].astype(jnp.bfloat16)
            keys = triple[HD : 2 * HD].astype(jnp.bfloat16)
            part = lax.dot_general(keys, queries, TN, preferred_element_type=jnp.float32)
            scores.append(jnp.where(same, part, -1e30))
        raised = [
            jnp.exp2((part - jnp.max(part, axis=0, keepdims=True)) * EXP2_SCALE) for part in scores
        ]
        for head in range(4):
            values = jnp.concatenate([triples[head][2 * HD : 192], triples[head][200:]], axis=0)
            total = jnp.sum(raised[head], axis=0, keepdims=True)
            mixed = jnp.dot(
                values.astype(jnp.bfloat16), raised[head].astype(jnp.bfloat16),
                preferred_element_type=jnp.float32,
            )
            mixed_ref[(step - 1) * 4 + head] = mixed / total

    @pl.when(step == pl.num_programs(0) - 1)
    def _():
        time_copy.wait()
        mixed = mixed_ref[...].reshape(-1, rows).astype(jnp.bfloat16)
        branch = lax.dot_general(mixed, time_table_ref[...], TN, preferred_element_type=jnp.float32)
        out_ref[...] = (
            middle_ref[...].astype(jnp.float32) + modulation_ref[1, 2:3] * branch
        ).astype(jnp.bfloat16)


def shards(tokens, frame_qkv, frame_out, time_qkv, time_out, modulation):
    tokens = tokens[0]
    rows, width = tokens.shape
    core = lax.axis_index("c")
    gathered = lax.all_gather(tokens, ("zh", "c"), axis=0, tiled=True)

    index = lax.axis_index("y") * 2 + core
    time_part = lax.dynamic_slice_in_dim(time_qkv, jnp.minimum(index * 32, 216 - 32), 32, 0)
    index = lax.axis_index("x") * 4 + lax.axis_index("y")
    out_part = lax.dynamic_slice_in_dim(frame_out, jnp.minimum(index, 8) * 16, 16, 0)
    time_parts = lax.all_gather(time_part, "zl", axis=0, tiled=True)
    out_parts = lax.all_gather(out_part, "zh", axis=0, tiled=True)
    parts = jnp.concatenate([time_parts, out_parts], axis=0)
    tables = lax.all_gather(parts, ("x", "y", "c"), axis=0)
    tables = tables.reshape(4, 8, 192, width)

    heads = frame_qkv.reshape(width, 2, 3, HD)
    wqk = jnp.pad(heads[:, :, :2], ((0, 0), (0, 0), (0, 0), (0, LANES - HD))).reshape(width, 4 * LANES)
    wvt = jnp.pad(jnp.transpose(heads[:, :, 2], (1, 2, 0)), ((0, 0), (0, HP - HD), (0, 0)))
    wvt = wvt.reshape(2 * HP, width)

    total = gathered.shape[0]
    mixed = pl.pallas_call(
        frame_kernel,
        out_shape=jax.ShapeDtypeStruct((total // LANES, 2 * HD, LANES), jnp.bfloat16),
        in_specs=[whole()] * 4,
        out_specs=whole(),
        scratch_shapes=[
            pltpu.VMEM((total, 4 * LANES), jnp.bfloat16),
            pltpu.VMEM((2 * HP, total), jnp.bfloat16),
        ],
        compiler_params=params(),
        name="frame_attention",
    )(gathered, modulation, wqk, wvt)

    mixed = lax.all_to_all(mixed, ("zh", "c"), 0, 0, tiled=True)
    joined = pl.pallas_call(
        join_kernel,
        out_shape=jax.ShapeDtypeStruct((rows, 2 * width), jnp.bfloat16),
        in_specs=[whole(), whole()],
        out_specs=whole(),
        compiler_params=params(),
        name="join",
    )(mixed, tokens)
    joined = lax.all_to_all(joined, ("x", "zl"), 0, 0, tiled=True)

    out = pl.pallas_call(
        functools.partial(time_kernel, rows // 16),
        grid=(5,),
        out_shape=jax.ShapeDtypeStruct((rows, width), jnp.bfloat16),
        in_specs=[
            whole(),
            pl.BlockSpec((1, 8, LANES, width), lambda i: (jnp.maximum(i - 1, 0), 0, 0, 0)),
            pl.BlockSpec(memory_space=pl.ANY),
            pl.BlockSpec(memory_space=pl.ANY),
            whole(),
        ],
        out_specs=whole(),
        scratch_shapes=[
            pltpu.VMEM((rows, width), jnp.bfloat16),
            pltpu.VMEM((rows, width), jnp.bfloat16),
            pltpu.VMEM((16, HD, rows), jnp.float32),
            pltpu.VMEM((8, 9, 16, width), jnp.bfloat16),
            pltpu.VMEM((width, width), jnp.bfloat16),
            pltpu.SemaphoreType.DMA((8,)),
            pltpu.SemaphoreType.DMA,
        ],
        compiler_params=params(),
        name="time_block",
    )(joined, tables, tables.reshape(16, 2, 192, width), time_out, modulation)
    out = lax.all_to_all(out, ("x", "zl"), 0, 0, tiled=True)
    return out[None]


def solution(mesh):
    fine = Mesh(mesh.devices.reshape(4, 4, 4, 4, 2), ("y", "x", "zl", "zh", "c"))
    frames, space = ("y", "x", "zl"), ("zh", "c")
    placed = (
        P(frames, space, None),
        P(None, space),
        P(space, None),
        P(("x", "zl"), None),
        P(),
        P("y", None, None),
    )
    return jax.shard_map(
        shards,
        mesh=fine,
        in_specs=placed,
        out_specs=P(frames, space, None),
        check_vma=False,
    )
```

```python
import functools
import math

import jax
import jax.numpy as jnp
from jax import lax
from jax.experimental import pallas as pl
from jax.experimental.pallas import tpu as pltpu
from jax.sharding import Mesh
from jax.sharding import PartitionSpec as P

HD = 72
HP = 80
LANES = 128
EPS = 1e-06
EXP2_SCALE = HD ** (-0.5) * math.log2(math.e)
NT = (((1,), (1,)), ((), ()))
TN = (((0,), (0,)), ((), ()))


def params(mib=48):
    return pltpu.CompilerParams(vmem_limit_bytes=mib * 1024 * 1024)


def whole():
    return pl.BlockSpec(memory_space=pltpu.VMEM)


def modulated(values, offset, stretch):
    center = jnp.mean(values, axis=-1, keepdims=True)
    values = values - center
    spread = jnp.mean(values * values, axis=-1, keepdims=True)
    return (values * lax.rsqrt(spread + EPS) * (1.0 + stretch) + offset).astype(jnp.bfloat16)


def triples_of(rows, modulation_ref, wqk_ref, wvt_ref):
    normed = modulated(rows, modulation_ref[0, 0:1], modulation_ref[0, 1:2])
    qk = lax.dot_general(normed, wqk_ref[...], NT, preferred_element_type=jnp.float32).astype(jnp.bfloat16)
    values = lax.dot_general(wvt_ref[...], normed, NT, preferred_element_type=jnp.float32)
    index = lax.broadcasted_iota(jnp.int32, values.shape, 0)
    ones = (index == HD) | (index == HP + HD)
    return qk, jnp.where(ones, 1.0, values).astype(jnp.bfloat16)


def spread_kernel(table_ref, wqk_ref, wvt_ref):
    table = table_ref[...].astype(jnp.float32)
    width = table.shape[1]
    wide, narrow = jnp.zeros((LANES - HD, width)), jnp.zeros((HP - HD, width))
    pieces = [table[HD * index : HD * index + HD] for index in range(6)]
    wqk_ref[...] = jnp.concatenate(
        [pieces[0], wide, pieces[1], wide, pieces[3], wide, pieces[4], wide], axis=0
    ).astype(jnp.bfloat16)
    wvt_ref[...] = jnp.concatenate([pieces[2], narrow, pieces[5], narrow], axis=0).astype(jnp.bfloat16)


def early_kernel(*refs):
    pieces, (modulation_ref, wqk_ref, wvt_ref, qk_ref, vt_ref) = refs[:-5], refs[-5:]
    for index in range(0, len(pieces), 2):
        rows = jnp.concatenate([pieces[index][...], pieces[index + 1][...]], axis=0)
        qk, vt = triples_of(rows.astype(jnp.float32), modulation_ref, wqk_ref, wvt_ref)
        start = LANES * index
        qk_ref[start : start + 2 * LANES] = qk
        vt_ref[:, start : start + 2 * LANES] = vt


def frame_kernel(
    place_ref, below_ref, above_ref, one_ref, two_ref, three_ref, four_ref, qk_ref, vt_ref, modulation_ref,
    wqk_ref, wvt_ref, out_ref, qk_late_ref, vt_late_ref,
):
    groups = ((below_ref, above_ref), (three_ref, four_ref, one_ref, two_ref))
    for index, group in enumerate(groups):
        rows = jnp.concatenate([ref[...] for ref in group], axis=0).astype(jnp.float32)
        qk, vt = triples_of(rows, modulation_ref, wqk_ref, wvt_ref)
        start = 2 * LANES * index
        qk_late_ref[start : start + 2 * LANES] = qk
        vt_late_ref[:, start : start + 2 * LANES] = vt
    parts = ((qk_ref, vt_ref), (qk_late_ref, vt_late_ref))
    blocks = (
        ((qk_ref, 0), (qk_ref, 128)),
        ((qk_ref, 256), (qk_late_ref, 0)),
        ((qk_ref, 384), (qk_late_ref, 128)),
        ((qk_late_ref, 384), (qk_late_ref, 256)),
    )
    for number, block in enumerate(blocks):
        outs = []
        for head in range(2):
            column = 2 * LANES * head
            queries = jnp.concatenate(
                [ref[start : start + LANES, column : column + LANES] for ref, start in block], axis=0
            )
            scores = [
                lax.dot_general(
                    qk[:, column + LANES : column + 2 * LANES], queries, NT,
                    preferred_element_type=jnp.float32,
                )
                for qk, _ in parts
            ]
            largest = jnp.maximum(*[jnp.max(part, axis=0, keepdims=True) for part in scores])
            mixed = sum(
                jnp.dot(
                    vt[HP * head : HP * head + HP],
                    jnp.exp2((part - largest) * EXP2_SCALE).astype(jnp.bfloat16),
                    preferred_element_type=jnp.float32,
                )
                for part, (_, vt) in zip(scores, parts)
            )
            outs.append(mixed[:HD] / mixed[HD : HD + 1])
        both = jnp.concatenate(outs, axis=0).astype(jnp.bfloat16)
        for part in range(2):
            out_ref[place_ref[2 * number + part]] = both[:, part * LANES : (part + 1) * LANES]


def middle_kernel(mixed_ref, tables_ref, tokens_ref, modulation_ref, out_ref, table_ref, sem):
    copy = pltpu.make_async_copy(tables_ref.at[pl.ds(0, 9), :, pl.ds(LANES, 64), :], table_ref, sem)
    copy.start()
    slots = [mixed_ref[2 * zh + core] for core in range(2) for zh in range(4)]
    mixed = jnp.concatenate(
        [slot[16 * number : 16 * number + 16] for number in range(9) for slot in slots], axis=0
    )
    copy.wait()
    table = table_ref[...].reshape(-1, table_ref.shape[-1])
    branch = lax.dot_general(mixed, table, TN, preferred_element_type=jnp.float32)
    out_ref[...] = (
        tokens_ref[...].astype(jnp.float32) + modulation_ref[0, 2:3] * branch
    ).astype(jnp.bfloat16)


def time_kernel(
    positions, middle_ref, tables_ref, out_table_ref, modulation_ref, out_ref,
    input_ref, mixed_ref, table_ref, sem,
):
    step = pl.program_id(0)
    copy = pltpu.make_async_copy(out_table_ref, table_ref, sem)

    @pl.when(step == 0)
    def _():
        copy.start()
        input_ref[...] = modulated(
            middle_ref[...].astype(jnp.float32), modulation_ref[1, 0:1], modulation_ref[1, 1:2]
        )

    rows, width = input_ref.shape
    one = lax.broadcasted_iota(jnp.int32, (rows, rows), 0) % positions
    two = lax.broadcasted_iota(jnp.int32, (rows, rows), 1) % positions
    same = one == two
    triples = []
    for slot in range(4):
        table = tables_ref[0, 0:7, 32 * slot : 32 * slot + 32].reshape(7 * 32, width)
        triples.append(lax.dot_general(table, input_ref[...], NT, preferred_element_type=jnp.float32))
    scores = []
    for triple in triples:
        queries = triple[:HD].astype(jnp.bfloat16)
        keys = triple[HD : 2 * HD].astype(jnp.bfloat16)
        part = lax.dot_general(keys, queries, TN, preferred_element_type=jnp.float32)
        scores.append(jnp.where(same, part, -1e30))
    raised = [
        jnp.exp2((part - jnp.max(part, axis=0, keepdims=True)) * EXP2_SCALE) for part in scores
    ]
    for slot in range(4):
        values = jnp.concatenate([triples[slot][2 * HD : 192], triples[slot][200:]], axis=0)
        total = jnp.sum(raised[slot], axis=0, keepdims=True)
        mixed = jnp.dot(
            values.astype(jnp.bfloat16), raised[slot].astype(jnp.bfloat16),
            preferred_element_type=jnp.float32,
        )
        mixed_ref[step * 4 + slot] = mixed / total

    @pl.when(step == pl.num_programs(0) - 1)
    def _():
        copy.wait()
        mixed = mixed_ref[...].reshape(-1, rows).astype(jnp.bfloat16)
        branch = lax.dot_general(mixed, table_ref[...], TN, preferred_element_type=jnp.float32)
        out_ref[...] = (
            middle_ref[...].astype(jnp.float32) + modulation_ref[1, 2:3] * branch
        ).astype(jnp.bfloat16)


def rotation(count, by):
    return [(index, (index + by) % count) for index in range(count)]


SWAP = [(0, 1), (1, 0)]


def shards(tokens, frame_qkv, frame_out, time_qkv, time_out, modulation):
    tokens = tokens[0]
    rows, width = tokens.shape
    half = rows // 2
    zh, core = lax.axis_index("zh"), lax.axis_index("c")

    def along(array, axis, by):
        return lax.ppermute(array, axis, rotation(4, by))

    def swapped(array):
        return lax.ppermute(array, "c", SWAP)

    before, after = along(tokens, "zh", 1), along(tokens, "zh", 3)
    beside = swapped(tokens)
    far_top, far_bottom = along(before[:half], "zh", 1), along(after[half:], "zh", 3)
    early = [tokens, beside, before, after]
    late = [swapped(before), swapped(after), far_top, far_bottom, swapped(far_top), swapped(far_bottom)]
    spots = [zh, (zh + 3) % 4, (zh + 1) % 4, (zh + 2) % 4]
    place = jnp.stack(
        [spot * 2 + side for spot in spots for side in (core, 1 - core)]
    ).astype(jnp.int32)

    index = lax.axis_index("y") * 2 + core
    time_part = lax.dynamic_slice_in_dim(time_qkv, jnp.minimum(index * 32, 216 - 32), 32, 0)
    index = lax.axis_index("x") * 4 + lax.axis_index("y")
    out_part = lax.dynamic_slice_in_dim(frame_out, jnp.minimum(index, 8) * 16, 16, 0)
    time_parts = lax.all_gather(time_part, "zl", axis=0, tiled=True)
    out_parts = lax.all_gather(out_part, "zh", axis=0, tiled=True)
    parts = [time_parts, out_parts]
    tables = lax.all_gather(jnp.concatenate(parts, axis=0), ("x", "y", "c"), axis=0)
    tables = tables.reshape(4, 8, 192, width)

    wqk, wvt = pl.pallas_call(
        spread_kernel,
        out_shape=(
            jax.ShapeDtypeStruct((4 * LANES, width), jnp.bfloat16),
            jax.ShapeDtypeStruct((2 * HP, width), jnp.bfloat16),
        ),
        in_specs=[whole()],
        out_specs=(whole(), whole()),
        compiler_params=params(),
        name="spread",
    )(frame_qkv.T)

    soon = rows * len(early)
    qk, vt = pl.pallas_call(
        early_kernel,
        out_shape=(
            jax.ShapeDtypeStruct((soon, 4 * LANES), jnp.bfloat16),
            jax.ShapeDtypeStruct((2 * HP, soon), jnp.bfloat16),
        ),
        in_specs=[whole()] * (len(early) + 3),
        out_specs=(whole(), whole()),
        compiler_params=params(),
        cost_estimate=pl.CostEstimate(flops=2 * 10**9, bytes_accessed=5 * 10**6, transcendentals=0),
        name="early_triples",
    )(*early, modulation, wqk, wvt)

    rest = 4 * rows
    mixed = pl.pallas_call(
        frame_kernel,
        out_shape=jax.ShapeDtypeStruct(((soon + rest) // LANES, 2 * HD, LANES), jnp.bfloat16),
        in_specs=[pl.BlockSpec(memory_space=pltpu.SMEM)] + [whole()] * 11,
        out_specs=whole(),
        scratch_shapes=[
            pltpu.VMEM((rest, 4 * LANES), jnp.bfloat16),
            pltpu.VMEM((2 * HP, rest), jnp.bfloat16),
        ],
        compiler_params=params(),
        name="frame_attention",
    )(place, *late, qk, vt, modulation, wqk, wvt)

    mixed = lax.all_to_all(mixed, ("zh", "c"), 0, 0, tiled=True)
    middle = pl.pallas_call(
        middle_kernel,
        out_shape=jax.ShapeDtypeStruct((rows, width), jnp.bfloat16),
        in_specs=[whole(), pl.BlockSpec(memory_space=pl.ANY), whole(), whole()],
        out_specs=whole(),
        scratch_shapes=[pltpu.VMEM((9, 2, 64, width), jnp.bfloat16), pltpu.SemaphoreType.DMA],
        compiler_params=params(),
        name="middle",
    )(mixed, tables.reshape(16, 2, 192, width), tokens, modulation)

    middle = lax.all_to_all(middle, ("x", "zl"), 0, 0, tiled=True)

    out = pl.pallas_call(
        functools.partial(time_kernel, rows // 16),
        grid=(4,),
        out_shape=jax.ShapeDtypeStruct((rows, width), jnp.bfloat16),
        in_specs=[
            whole(),
            pl.BlockSpec((1, 8, LANES, width), lambda i: (i, 0, 0, 0)),
            pl.BlockSpec(memory_space=pl.ANY),
            whole(),
        ],
        out_specs=whole(),
        scratch_shapes=[
            pltpu.VMEM((rows, width), jnp.bfloat16),
            pltpu.VMEM((16, HD, rows), jnp.float32),
            pltpu.VMEM((width, width), jnp.bfloat16),
            pltpu.SemaphoreType.DMA,
        ],
        compiler_params=params(),
        name="time_block",
    )(middle, tables, time_out, modulation)
    out = lax.all_to_all(out, ("x", "zl"), 0, 0, tiled=True)
    return out[None]


def solution(mesh):
    fine = Mesh(mesh.devices.reshape(4, 4, 4, 4, 2), ("y", "x", "zl", "zh", "c"))
    frames, space = ("y", "x", "zl"), ("zh", "c")
    placed = (
        P(frames, space, None),
        P(None, space),
        P(space, None),
        P(("x", "zl"), None),
        P(),
        P("y", None, None),
    )
    return jax.shard_map(
        shards,
        mesh=fine,
        in_specs=placed,
        out_specs=P(frames, space, None),
        check_vma=False,
    )
```

```python
import functools
import math

import jax
import jax.numpy as jnp
from jax import lax
from jax.experimental import pallas as pl
from jax.experimental.pallas import tpu as pltpu
from jax.sharding import Mesh
from jax.sharding import PartitionSpec as P

HD = 72
HP = 80
LANES = 128
EPS = 1e-06
EXP2_SCALE = HD ** (-0.5) * math.log2(math.e)
NT = (((1,), (1,)), ((), ()))
TN = (((0,), (0,)), ((), ()))


def params(mib=48):
    return pltpu.CompilerParams(vmem_limit_bytes=mib * 1024 * 1024)


def whole():
    return pl.BlockSpec(memory_space=pltpu.VMEM)


def modulated(values, offset, stretch):
    center = jnp.mean(values, axis=-1, keepdims=True)
    values = values - center
    spread = jnp.mean(values * values, axis=-1, keepdims=True)
    return (values * lax.rsqrt(spread + EPS) * (1.0 + stretch) + offset).astype(jnp.bfloat16)


def triples_of(rows, modulation_ref, wqk_ref, wvt_ref):
    normed = modulated(rows, modulation_ref[0, 0:1], modulation_ref[0, 1:2])
    qk = lax.dot_general(normed, wqk_ref[...], NT, preferred_element_type=jnp.float32).astype(jnp.bfloat16)
    values = lax.dot_general(wvt_ref[...], normed, NT, preferred_element_type=jnp.float32)
    index = lax.broadcasted_iota(jnp.int32, values.shape, 0)
    ones = (index == HD) | (index == HP + HD)
    return qk, jnp.where(ones, 1.0, values).astype(jnp.bfloat16)


def spread_kernel(table_ref, wqk_ref, wvt_ref):
    table = table_ref[...].astype(jnp.float32)
    width = table.shape[1]
    wide, narrow = jnp.zeros((LANES - HD, width)), jnp.zeros((HP - HD, width))
    pieces = [table[HD * index : HD * index + HD] for index in range(6)]
    wqk_ref[...] = jnp.concatenate(
        [pieces[0], wide, pieces[1], wide, pieces[3], wide, pieces[4], wide], axis=0
    ).astype(jnp.bfloat16)
    wvt_ref[...] = jnp.concatenate([pieces[2], narrow, pieces[5], narrow], axis=0).astype(jnp.bfloat16)


def early_kernel(*refs):
    pieces, (modulation_ref, wqk_ref, wvt_ref, qk_ref, vt_ref) = refs[:-5], refs[-5:]
    for index in range(0, len(pieces), 2):
        rows = jnp.concatenate([pieces[index][...], pieces[index + 1][...]], axis=0)
        qk, vt = triples_of(rows.astype(jnp.float32), modulation_ref, wqk_ref, wvt_ref)
        start = LANES * index
        qk_ref[start : start + 2 * LANES] = qk
        vt_ref[:, start : start + 2 * LANES] = vt


def frame_kernel(
    place_ref, below_ref, above_ref, one_ref, two_ref, three_ref, four_ref, qk_ref, vt_ref, modulation_ref,
    wqk_ref, wvt_ref, out_ref, qk_late_ref, vt_late_ref,
):
    groups = ((below_ref, above_ref), (three_ref, four_ref, one_ref, two_ref))
    for index, group in enumerate(groups):
        rows = jnp.concatenate([ref[...] for ref in group], axis=0).astype(jnp.float32)
        qk, vt = triples_of(rows, modulation_ref, wqk_ref, wvt_ref)
        start = 2 * LANES * index
        qk_late_ref[start : start + 2 * LANES] = qk
        vt_late_ref[:, start : start + 2 * LANES] = vt
    parts = ((qk_ref, vt_ref), (qk_late_ref, vt_late_ref))
    blocks = (
        ((qk_ref, 0), (qk_ref, 128)),
        ((qk_ref, 256), (qk_late_ref, 0)),
        ((qk_ref, 384), (qk_late_ref, 128)),
        ((qk_late_ref, 384), (qk_late_ref, 256)),
    )
    for number, block in enumerate(blocks):
        outs = []
        for head in range(2):
            column = 2 * LANES * head
            queries = jnp.concatenate(
                [ref[start : start + LANES, column : column + LANES] for ref, start in block], axis=0
            )
            scores = [
                lax.dot_general(
                    qk[:, column + LANES : column + 2 * LANES], queries, NT,
                    preferred_element_type=jnp.float32,
                )
                for qk, _ in parts
            ]
            largest = jnp.maximum(*[jnp.max(part, axis=0, keepdims=True) for part in scores])
            mixed = sum(
                jnp.dot(
                    vt[HP * head : HP * head + HP],
                    jnp.exp2((part - largest) * EXP2_SCALE).astype(jnp.bfloat16),
                    preferred_element_type=jnp.float32,
                )
                for part, (_, vt) in zip(scores, parts)
            )
            outs.append(mixed[:HD] / mixed[HD : HD + 1])
        both = jnp.concatenate(outs, axis=0).astype(jnp.bfloat16)
        for part in range(2):
            out_ref[place_ref[2 * number + part]] = both[:, part * LANES : (part + 1) * LANES]


def pack_kernel(parts_ref, below_ref, above_ref, out_ref):
    parts = parts_ref[...].astype(jnp.float32)
    rows = [parts[16 * (4 * zh + zl) : 16 * (4 * zh + zl) + 8] for zl in range(4) for zh in range(4)]
    rows += [parts[16 * (4 * zh + zl) + 8 : 16 * (4 * zh + zl) + 16] for zh in range(4) for zl in range(2)]
    out_ref[...] = jnp.concatenate(rows, axis=0).astype(jnp.bfloat16)


def join_kernel(mixed_ref, tokens_ref, out_ref):
    width = tokens_ref.shape[1]
    mixed = mixed_ref[...].reshape(-1, LANES).astype(jnp.float32)
    out_ref[:, :width] = mixed.T.astype(jnp.bfloat16)
    out_ref[:, width:] = tokens_ref[...]


def time_kernel(
    positions, joined_ref, tables_ref, all_ref, out_table_ref, modulation_ref, out_ref,
    middle_ref, input_ref, mixed_ref, frame_table_ref, time_table_ref, frame_sem, time_sem,
):
    step = pl.program_id(0)
    rows, width = input_ref.shape
    time_copy = pltpu.make_async_copy(out_table_ref, time_table_ref, time_sem)

    @pl.when(step == 0)
    def _():
        frame_copies = [
            pltpu.make_async_copy(
                all_ref.at[pl.ds(0, 9), core, pl.ds(LANES + 16 * zh, 16), :],
                frame_table_ref.at[2 * zh + core],
                frame_sem.at[2 * zh + core],
            )
            for zh in range(4)
            for core in range(2)
        ]
        for copy in frame_copies:
            copy.start()
        time_copy.start()
        for copy in frame_copies:
            copy.wait()
        table = frame_table_ref[...].reshape(width, width)
        branch = jnp.dot(joined_ref[:, :width], table, preferred_element_type=jnp.float32)
        middle = joined_ref[:, width:].astype(jnp.float32) + modulation_ref[0, 2:3] * branch
        middle = middle.astype(jnp.bfloat16)
        middle_ref[...] = middle
        input_ref[...] = modulated(
            middle.astype(jnp.float32), modulation_ref[1, 0:1], modulation_ref[1, 1:2]
        )

    @pl.when(step > 0)
    def _():
        one = lax.broadcasted_iota(jnp.int32, (rows, rows), 0) % positions
        two = lax.broadcasted_iota(jnp.int32, (rows, rows), 1) % positions
        same = one == two
        triples = []
        for head in range(4):
            table = tables_ref[0, 0:7, 32 * head : 32 * head + 32].reshape(7 * 32, width)
            triples.append(
                lax.dot_general(table, input_ref[...], NT, preferred_element_type=jnp.float32)
            )
        scores = []
        for triple in triples:
            queries = triple[:HD].astype(jnp.bfloat16)
            keys = triple[HD : 2 * HD].astype(jnp.bfloat16)
            part = lax.dot_general(keys, queries, TN, preferred_element_type=jnp.float32)
            scores.append(jnp.where(same, part, -1e30))
        raised = [
            jnp.exp2((part - jnp.max(part, axis=0, keepdims=True)) * EXP2_SCALE) for part in scores
        ]
        for head in range(4):
            values = jnp.concatenate([triples[head][2 * HD : 192], triples[head][200:]], axis=0)
            total = jnp.sum(raised[head], axis=0, keepdims=True)
            mixed = jnp.dot(
                values.astype(jnp.bfloat16), raised[head].astype(jnp.bfloat16),
                preferred_element_type=jnp.float32,
            )
            mixed_ref[(step - 1) * 4 + head] = mixed / total

    @pl.when(step == pl.num_programs(0) - 1)
    def _():
        time_copy.wait()
        mixed = mixed_ref[...].reshape(-1, rows).astype(jnp.bfloat16)
        branch = lax.dot_general(mixed, time_table_ref[...], TN, preferred_element_type=jnp.float32)
        out_ref[...] = (
            middle_ref[...].astype(jnp.float32) + modulation_ref[1, 2:3] * branch
        ).astype(jnp.bfloat16)


def rotation(count, by):
    return [(index, (index + by) % count) for index in range(count)]


SWAP = [(0, 1), (1, 0)]


def shards(tokens, frame_qkv, frame_out, time_qkv, time_out, modulation):
    tokens = tokens[0]
    rows, width = tokens.shape
    half = rows // 2
    zh, core = lax.axis_index("zh"), lax.axis_index("c")

    def along(array, axis, by):
        return lax.ppermute(array, axis, rotation(4, by))

    def swapped(array):
        return lax.ppermute(array, "c", SWAP)

    x, y, zl = lax.axis_index("x"), lax.axis_index("y"), lax.axis_index("zl")
    start = jnp.minimum(32 * (2 * y + core), 216 - 32) + 8 * zh
    time_part = lax.dynamic_slice_in_dim(time_qkv, start, 8, 0)
    start = 16 * jnp.minimum(4 * x + y, 8) + 8 * (zl % 2)
    out_part = lax.dynamic_slice_in_dim(frame_out, start, 8, 0)
    part = jnp.concatenate([time_part, out_part], axis=0)
    parts = lax.all_gather(part, ("zh", "zl"), axis=0, tiled=True)

    before, after = along(tokens, "zh", 1), along(tokens, "zh", 3)
    beside = swapped(tokens)
    parts = pl.pallas_call(
        pack_kernel,
        out_shape=jax.ShapeDtypeStruct((4 * 32 + 4 * 16, width), parts.dtype),
        in_specs=[whole(), pl.BlockSpec(memory_space=pl.ANY), pl.BlockSpec(memory_space=pl.ANY)],
        out_specs=whole(),
        compiler_params=params(),
        name="pack",
    )(parts, before, after)
    tables = lax.all_gather(parts, ("x", "y", "c"), axis=0)
    far_top, far_bottom = along(before[:half], "zh", 1), along(after[half:], "zh", 3)
    early = [tokens, beside, before, after]
    late = [swapped(before), swapped(after), far_top, far_bottom, swapped(far_top), swapped(far_bottom)]
    spots = [zh, (zh + 3) % 4, (zh + 1) % 4, (zh + 2) % 4]
    place = jnp.stack([spot * 2 + side for spot in spots for side in (core, 1 - core)]).astype(jnp.int32)

    tables = tables.reshape(4, 8, 192, width)

    wqk, wvt = pl.pallas_call(
        spread_kernel,
        out_shape=(
            jax.ShapeDtypeStruct((4 * LANES, width), jnp.bfloat16),
            jax.ShapeDtypeStruct((2 * HP, width), jnp.bfloat16),
        ),
        in_specs=[whole()],
        out_specs=(whole(), whole()),
        compiler_params=params(),
        name="spread",
    )(frame_qkv.T)

    soon = rows * len(early)
    qk, vt = pl.pallas_call(
        early_kernel,
        out_shape=(
            jax.ShapeDtypeStruct((soon, 4 * LANES), jnp.bfloat16),
            jax.ShapeDtypeStruct((2 * HP, soon), jnp.bfloat16),
        ),
        in_specs=[whole()] * (len(early) + 3),
        out_specs=(whole(), whole()),
        compiler_params=params(),
        cost_estimate=pl.CostEstimate(flops=2 * 10**9, bytes_accessed=5 * 10**6, transcendentals=0),
        name="early_triples",
    )(*early, modulation, wqk, wvt)

    rest = 4 * rows
    mixed = pl.pallas_call(
        frame_kernel,
        out_shape=jax.ShapeDtypeStruct(((soon + rest) // LANES, 2 * HD, LANES), jnp.bfloat16),
        in_specs=[pl.BlockSpec(memory_space=pltpu.SMEM)] + [whole()] * 11,
        out_specs=whole(),
        scratch_shapes=[
            pltpu.VMEM((rest, 4 * LANES), jnp.bfloat16),
            pltpu.VMEM((2 * HP, rest), jnp.bfloat16),
        ],
        compiler_params=params(),
        name="frame_attention",
    )(place, *late, qk, vt, modulation, wqk, wvt)

    mixed = lax.all_to_all(mixed, ("zh", "c"), 0, 0, tiled=True)
    joined = pl.pallas_call(
        join_kernel,
        out_shape=jax.ShapeDtypeStruct((rows, 2 * width), jnp.bfloat16),
        in_specs=[whole(), whole()],
        out_specs=whole(),
        compiler_params=params(),
        name="join",
    )(mixed, tokens)
    joined = lax.all_to_all(joined, ("x", "zl"), 0, 0, tiled=True)

    out = pl.pallas_call(
        functools.partial(time_kernel, rows // 16),
        grid=(5,),
        out_shape=jax.ShapeDtypeStruct((rows, width), jnp.bfloat16),
        in_specs=[
            whole(),
            pl.BlockSpec((1, 8, LANES, width), lambda i: (jnp.maximum(i - 1, 0), 0, 0, 0)),
            pl.BlockSpec(memory_space=pl.ANY),
            pl.BlockSpec(memory_space=pl.ANY),
            whole(),
        ],
        out_specs=whole(),
        scratch_shapes=[
            pltpu.VMEM((rows, width), jnp.bfloat16),
            pltpu.VMEM((rows, width), jnp.bfloat16),
            pltpu.VMEM((16, HD, rows), jnp.float32),
            pltpu.VMEM((8, 9, 16, width), jnp.bfloat16),
            pltpu.VMEM((width, width), jnp.bfloat16),
            pltpu.SemaphoreType.DMA((8,)),
            pltpu.SemaphoreType.DMA,
        ],
        compiler_params=params(),
        name="time_block",
    )(joined, tables, tables.reshape(16, 2, 192, width), time_out, modulation)
    out = lax.all_to_all(out, ("x", "zl"), 0, 0, tiled=True)
    return out[None]


def solution(mesh):
    fine = Mesh(mesh.devices.reshape(4, 4, 4, 4, 2), ("y", "x", "zl", "zh", "c"))
    frames, space = ("y", "x", "zl"), ("zh", "c")
    placed = (
        P(frames, space, None),
        P(None, space),
        P(space, None),
        P(("x", "zl"), None),
        P(),
        P("y", None, None),
    )
    return jax.shard_map(
        shards,
        mesh=fine,
        in_specs=placed,
        out_specs=P(frames, space, None),
        check_vma=False,
    )
```

```python
import functools
import math

import jax
import jax.numpy as jnp
from jax import lax
from jax.experimental import pallas as pl
from jax.experimental.pallas import tpu as pltpu
from jax.sharding import Mesh
from jax.sharding import PartitionSpec as P

HD = 72
HP = 80
LANES = 128
EPS = 1e-06
EXP2_SCALE = HD ** (-0.5) * math.log2(math.e)
NT = (((1,), (1,)), ((), ()))
TN = (((0,), (0,)), ((), ()))


def params(mib=48):
    return pltpu.CompilerParams(vmem_limit_bytes=mib * 1024 * 1024)


def whole():
    return pl.BlockSpec(memory_space=pltpu.VMEM)


def modulated(values, offset, stretch):
    center = jnp.mean(values, axis=-1, keepdims=True)
    values = values - center
    spread = jnp.mean(values * values, axis=-1, keepdims=True)
    return (values * lax.rsqrt(spread + EPS) * (1.0 + stretch) + offset).astype(jnp.bfloat16)


def triples_of(rows, modulation_ref, wqk_ref, wvt_ref):
    normed = modulated(rows, modulation_ref[0, 0:1], modulation_ref[0, 1:2])
    qk = lax.dot_general(normed, wqk_ref[...], NT, preferred_element_type=jnp.float32).astype(jnp.bfloat16)
    values = lax.dot_general(wvt_ref[...], normed, NT, preferred_element_type=jnp.float32)
    index = lax.broadcasted_iota(jnp.int32, values.shape, 0)
    ones = (index == HD) | (index == HP + HD)
    return qk, jnp.where(ones, 1.0, values).astype(jnp.bfloat16)


def spread_kernel(table_ref, wqk_ref, wvt_ref):
    table = table_ref[...].astype(jnp.float32)
    width = table.shape[1]
    wide, narrow = jnp.zeros((LANES - HD, width)), jnp.zeros((HP - HD, width))
    pieces = [table[HD * index : HD * index + HD] for index in range(6)]
    wqk_ref[...] = jnp.concatenate(
        [pieces[0], wide, pieces[1], wide, pieces[3], wide, pieces[4], wide], axis=0
    ).astype(jnp.bfloat16)
    wvt_ref[...] = jnp.concatenate([pieces[2], narrow, pieces[5], narrow], axis=0).astype(jnp.bfloat16)


def early_kernel(*refs):
    pieces, (modulation_ref, wqk_ref, wvt_ref, qk_ref, vt_ref) = refs[:-5], refs[-5:]
    for index in range(0, len(pieces), 2):
        rows = jnp.concatenate([pieces[index][...], pieces[index + 1][...]], axis=0)
        qk, vt = triples_of(rows.astype(jnp.float32), modulation_ref, wqk_ref, wvt_ref)
        start = LANES * index
        qk_ref[start : start + 2 * LANES] = qk
        vt_ref[:, start : start + 2 * LANES] = vt


def frame_kernel(
    place_ref, below_ref, above_ref, one_ref, two_ref, three_ref, four_ref, qk_ref, vt_ref, modulation_ref,
    wqk_ref, wvt_ref, out_ref, qk_late_ref, vt_late_ref,
):
    groups = ((below_ref, above_ref), (three_ref, four_ref, one_ref, two_ref))
    for index, group in enumerate(groups):
        rows = jnp.concatenate([ref[...] for ref in group], axis=0).astype(jnp.float32)
        qk, vt = triples_of(rows, modulation_ref, wqk_ref, wvt_ref)
        start = 2 * LANES * index
        qk_late_ref[start : start + 2 * LANES] = qk
        vt_late_ref[:, start : start + 2 * LANES] = vt
    parts = ((qk_ref, vt_ref), (qk_late_ref, vt_late_ref))
    blocks = (
        ((qk_ref, 0), (qk_ref, 128)),
        ((qk_ref, 256), (qk_late_ref, 0)),
        ((qk_ref, 384), (qk_late_ref, 128)),
        ((qk_late_ref, 384), (qk_late_ref, 256)),
    )
    for number, block in enumerate(blocks):
        outs = []
        for head in range(2):
            column = 2 * LANES * head
            queries = jnp.concatenate(
                [ref[start : start + LANES, column : column + LANES] for ref, start in block], axis=0
            )
            scores = [
                lax.dot_general(
                    qk[:, column + LANES : column + 2 * LANES], queries, NT,
                    preferred_element_type=jnp.float32,
                )
                for qk, _ in parts
            ]
            largest = jnp.maximum(*[jnp.max(part, axis=0, keepdims=True) for part in scores])
            mixed = sum(
                jnp.dot(
                    vt[HP * head : HP * head + HP],
                    jnp.exp2((part - largest) * EXP2_SCALE).astype(jnp.bfloat16),
                    preferred_element_type=jnp.float32,
                )
                for part, (_, vt) in zip(scores, parts)
            )
            outs.append(mixed[:HD] / mixed[HD : HD + 1])
        both = jnp.concatenate(outs, axis=0).astype(jnp.bfloat16)
        for part in range(2):
            out_ref[place_ref[2 * number + part]] = both[:, part * LANES : (part + 1) * LANES]


def pack_kernel(parts_ref, out_ref):
    parts = parts_ref[...].astype(jnp.float32)
    rows = [parts[16 * (4 * zh + zl) : 16 * (4 * zh + zl) + 8] for zl in range(4) for zh in range(4)]
    rows += [parts[16 * (4 * zh + zl) + 8 : 16 * (4 * zh + zl) + 16] for zh in range(4) for zl in range(2)]
    out_ref[...] = jnp.concatenate(rows, axis=0).astype(jnp.bfloat16)


def middle_kernel(mixed_ref, tables_ref, tokens_ref, modulation_ref, out_ref, table_ref, sem):
    copy = pltpu.make_async_copy(tables_ref.at[pl.ds(0, 9), :, pl.ds(LANES, 64), :], table_ref, sem)
    copy.start()
    slots = [mixed_ref[2 * zh + core] for core in range(2) for zh in range(4)]
    mixed = jnp.concatenate(
        [slot[16 * number : 16 * number + 16] for number in range(9) for slot in slots], axis=0
    )
    copy.wait()
    table = table_ref[...].reshape(-1, table_ref.shape[-1])
    branch = lax.dot_general(mixed, table, TN, preferred_element_type=jnp.float32)
    out_ref[...] = (
        tokens_ref[...].astype(jnp.float32) + modulation_ref[0, 2:3] * branch
    ).astype(jnp.bfloat16)


def time_kernel(
    positions, middle_ref, tables_ref, out_table_ref, modulation_ref, out_ref,
    input_ref, mixed_ref, table_ref, sem,
):
    step = pl.program_id(0)
    copy = pltpu.make_async_copy(out_table_ref, table_ref, sem)

    @pl.when(step == 0)
    def _():
        copy.start()
        input_ref[...] = modulated(
            middle_ref[...].astype(jnp.float32), modulation_ref[1, 0:1], modulation_ref[1, 1:2]
        )

    rows, width = input_ref.shape
    one = lax.broadcasted_iota(jnp.int32, (rows, rows), 0) % positions
    two = lax.broadcasted_iota(jnp.int32, (rows, rows), 1) % positions
    same = one == two
    triples = []
    for slot in range(4):
        table = tables_ref[0, 0:7, 32 * slot : 32 * slot + 32].reshape(7 * 32, width)
        triples.append(lax.dot_general(table, input_ref[...], NT, preferred_element_type=jnp.float32))
    scores = []
    for triple in triples:
        queries = triple[:HD].astype(jnp.bfloat16)
        keys = triple[HD : 2 * HD].astype(jnp.bfloat16)
        part = lax.dot_general(keys, queries, TN, preferred_element_type=jnp.float32)
        scores.append(jnp.where(same, part, -1e30))
    raised = [
        jnp.exp2((part - jnp.max(part, axis=0, keepdims=True)) * EXP2_SCALE) for part in scores
    ]
    for slot in range(4):
        values = jnp.concatenate([triples[slot][2 * HD : 192], triples[slot][200:]], axis=0)
        total = jnp.sum(raised[slot], axis=0, keepdims=True)
        mixed = jnp.dot(
            values.astype(jnp.bfloat16), raised[slot].astype(jnp.bfloat16),
            preferred_element_type=jnp.float32,
        )
        mixed_ref[step * 4 + slot] = mixed / total

    @pl.when(step == pl.num_programs(0) - 1)
    def _():
        copy.wait()
        mixed = mixed_ref[...].reshape(-1, rows).astype(jnp.bfloat16)
        branch = lax.dot_general(mixed, table_ref[...], TN, preferred_element_type=jnp.float32)
        out_ref[...] = (
            middle_ref[...].astype(jnp.float32) + modulation_ref[1, 2:3] * branch
        ).astype(jnp.bfloat16)


def rotation(count, by):
    return [(index, (index + by) % count) for index in range(count)]


SWAP = [(0, 1), (1, 0)]


def shards(tokens, frame_qkv, frame_out, time_qkv, time_out, modulation):
    tokens = tokens[0]
    rows, width = tokens.shape
    half = rows // 2
    zh, core = lax.axis_index("zh"), lax.axis_index("c")

    def along(array, axis, by):
        return lax.ppermute(array, axis, rotation(4, by))

    def swapped(array):
        return lax.ppermute(array, "c", SWAP)

    before, after = along(tokens, "zh", 1), along(tokens, "zh", 3)
    beside = swapped(tokens)
    far_top, far_bottom = along(before[:half], "zh", 1), along(after[half:], "zh", 3)
    early = [tokens, beside, before, after]
    late = [swapped(before), swapped(after), far_top, far_bottom, swapped(far_top), swapped(far_bottom)]
    spots = [zh, (zh + 3) % 4, (zh + 1) % 4, (zh + 2) % 4]
    place = jnp.stack(
        [spot * 2 + side for spot in spots for side in (core, 1 - core)]
    ).astype(jnp.int32)

    x, y, zl = lax.axis_index("x"), lax.axis_index("y"), lax.axis_index("zl")
    start = jnp.minimum(32 * (2 * y + core), 216 - 32) + 8 * zh
    time_part = lax.dynamic_slice_in_dim(time_qkv, start, 8, 0)
    start = 16 * jnp.minimum(4 * x + y, 8) + 8 * (zl % 2)
    out_part = lax.dynamic_slice_in_dim(frame_out, start, 8, 0)
    part = jnp.concatenate([time_part, out_part], axis=0)
    parts = lax.all_gather(part, ("zh", "zl"), axis=0, tiled=True)
    parts = pl.pallas_call(
        pack_kernel,
        out_shape=jax.ShapeDtypeStruct((4 * 32 + 4 * 16, width), parts.dtype),
        in_specs=[whole()],
        out_specs=whole(),
        compiler_params=params(),
        name="pack",
    )(parts)
    tables = lax.all_gather(parts, ("x", "y", "c"), axis=0)
    tables = tables.reshape(4, 8, 192, width)

    wqk, wvt = pl.pallas_call(
        spread_kernel,
        out_shape=(
            jax.ShapeDtypeStruct((4 * LANES, width), jnp.bfloat16),
            jax.ShapeDtypeStruct((2 * HP, width), jnp.bfloat16),
        ),
        in_specs=[whole()],
        out_specs=(whole(), whole()),
        compiler_params=params(),
        name="spread",
    )(frame_qkv.T)

    soon = rows * len(early)
    qk, vt = pl.pallas_call(
        early_kernel,
        out_shape=(
            jax.ShapeDtypeStruct((soon, 4 * LANES), jnp.bfloat16),
            jax.ShapeDtypeStruct((2 * HP, soon), jnp.bfloat16),
        ),
        in_specs=[whole()] * (len(early) + 3),
        out_specs=(whole(), whole()),
        compiler_params=params(),
        cost_estimate=pl.CostEstimate(flops=2 * 10**9, bytes_accessed=5 * 10**6, transcendentals=0),
        name="early_triples",
    )(*early, modulation, wqk, wvt)

    rest = 4 * rows
    mixed = pl.pallas_call(
        frame_kernel,
        out_shape=jax.ShapeDtypeStruct(((soon + rest) // LANES, 2 * HD, LANES), jnp.bfloat16),
        in_specs=[pl.BlockSpec(memory_space=pltpu.SMEM)] + [whole()] * 11,
        out_specs=whole(),
        scratch_shapes=[
            pltpu.VMEM((rest, 4 * LANES), jnp.bfloat16),
            pltpu.VMEM((2 * HP, rest), jnp.bfloat16),
        ],
        compiler_params=params(),
        name="frame_attention",
    )(place, *late, qk, vt, modulation, wqk, wvt)

    mixed = lax.all_to_all(mixed, ("zh", "c"), 0, 0, tiled=True)
    middle = pl.pallas_call(
        middle_kernel,
        out_shape=jax.ShapeDtypeStruct((rows, width), jnp.bfloat16),
        in_specs=[whole(), pl.BlockSpec(memory_space=pl.ANY), whole(), whole()],
        out_specs=whole(),
        scratch_shapes=[pltpu.VMEM((9, 2, 64, width), jnp.bfloat16), pltpu.SemaphoreType.DMA],
        compiler_params=params(),
        name="middle",
    )(mixed, tables.reshape(16, 2, 192, width), tokens, modulation)

    middle = lax.all_to_all(middle, ("x", "zl"), 0, 0, tiled=True)

    out = pl.pallas_call(
        functools.partial(time_kernel, rows // 16),
        grid=(4,),
        out_shape=jax.ShapeDtypeStruct((rows, width), jnp.bfloat16),
        in_specs=[
            whole(),
            pl.BlockSpec((1, 8, LANES, width), lambda i: (i, 0, 0, 0)),
            pl.BlockSpec(memory_space=pl.ANY),
            whole(),
        ],
        out_specs=whole(),
        scratch_shapes=[
            pltpu.VMEM((rows, width), jnp.bfloat16),
            pltpu.VMEM((16, HD, rows), jnp.float32),
            pltpu.VMEM((width, width), jnp.bfloat16),
            pltpu.SemaphoreType.DMA,
        ],
        compiler_params=params(),
        name="time_block",
    )(middle, tables, time_out, modulation)
    out = lax.all_to_all(out, ("x", "zl"), 0, 0, tiled=True)
    return out[None]


def solution(mesh):
    fine = Mesh(mesh.devices.reshape(4, 4, 4, 4, 2), ("y", "x", "zl", "zh", "c"))
    frames, space = ("y", "x", "zl"), ("zh", "c")
    placed = (
        P(frames, space, None),
        P(None, space),
        P(space, None),
        P(("x", "zl"), None),
        P(),
        P("y", None, None),
    )
    return jax.shard_map(
        shards,
        mesh=fine,
        in_specs=placed,
        out_specs=P(frames, space, None),
        check_vma=False,
    )
```

```python
import functools
import math

import jax
import jax.numpy as jnp
from jax import lax
from jax.experimental import pallas as pl
from jax.experimental.pallas import tpu as pltpu
from jax.sharding import Mesh
from jax.sharding import PartitionSpec as P

HD = 72
HP = 80
LANES = 128
EPS = 1e-06
EXP2_SCALE = HD ** (-0.5) * math.log2(math.e)
NT = (((1,), (1,)), ((), ()))
TN = (((0,), (0,)), ((), ()))


def params(mib=48):
    return pltpu.CompilerParams(vmem_limit_bytes=mib * 1024 * 1024)


def whole():
    return pl.BlockSpec(memory_space=pltpu.VMEM)


def modulated(values, offset, stretch):
    center = jnp.mean(values, axis=-1, keepdims=True)
    values = values - center
    spread = jnp.mean(values * values, axis=-1, keepdims=True)
    return (values * lax.rsqrt(spread + EPS) * (1.0 + stretch) + offset).astype(jnp.bfloat16)


def triples_of(rows, modulation_ref, wqk_ref, wvt_ref):
    normed = modulated(rows, modulation_ref[0, 0:1], modulation_ref[0, 1:2])
    qk = lax.dot_general(normed, wqk_ref[...], NT, preferred_element_type=jnp.float32).astype(jnp.bfloat16)
    values = lax.dot_general(wvt_ref[...], normed, NT, preferred_element_type=jnp.float32)
    index = lax.broadcasted_iota(jnp.int32, values.shape, 0)
    ones = (index == HD) | (index == HP + HD)
    return qk, jnp.where(ones, 1.0, values).astype(jnp.bfloat16)


def spread_kernel(table_ref, wqk_ref, wvt_ref):
    table = table_ref[...].astype(jnp.float32)
    width = table.shape[1]
    wide, narrow = jnp.zeros((LANES - HD, width)), jnp.zeros((HP - HD, width))
    pieces = [table[HD * index : HD * index + HD] for index in range(6)]
    wqk_ref[...] = jnp.concatenate(
        [pieces[0], wide, pieces[1], wide, pieces[3], wide, pieces[4], wide], axis=0
    ).astype(jnp.bfloat16)
    wvt_ref[...] = jnp.concatenate([pieces[2], narrow, pieces[5], narrow], axis=0).astype(jnp.bfloat16)


def early_kernel(*refs):
    pieces, (modulation_ref, wqk_ref, wvt_ref, qk_ref, vt_ref) = refs[:-5], refs[-5:]
    for index in range(0, len(pieces), 2):
        rows = jnp.concatenate([pieces[index][...], pieces[index + 1][...]], axis=0)
        qk, vt = triples_of(rows.astype(jnp.float32), modulation_ref, wqk_ref, wvt_ref)
        start = LANES * index
        qk_ref[start : start + 2 * LANES] = qk
        vt_ref[:, start : start + 2 * LANES] = vt


def frame_kernel(
    place_ref, below_ref, above_ref, one_ref, two_ref, three_ref, four_ref, qk_ref, vt_ref, modulation_ref,
    wqk_ref, wvt_ref, out_ref, qk_late_ref, vt_late_ref,
):
    groups = ((below_ref, above_ref), (three_ref, four_ref, one_ref, two_ref))
    for index, group in enumerate(groups):
        rows = jnp.concatenate([ref[...] for ref in group], axis=0).astype(jnp.float32)
        qk, vt = triples_of(rows, modulation_ref, wqk_ref, wvt_ref)
        start = 2 * LANES * index
        qk_late_ref[start : start + 2 * LANES] = qk
        vt_late_ref[:, start : start + 2 * LANES] = vt
    parts = ((qk_ref, vt_ref), (qk_late_ref, vt_late_ref))
    blocks = (
        ((qk_ref, 0), (qk_ref, 128)),
        ((qk_ref, 256), (qk_late_ref, 0)),
        ((qk_ref, 384), (qk_late_ref, 128)),
        ((qk_late_ref, 384), (qk_late_ref, 256)),
    )
    for number, block in enumerate(blocks):
        outs = []
        for head in range(2):
            column = 2 * LANES * head
            queries = jnp.concatenate(
                [ref[start : start + LANES, column : column + LANES] for ref, start in block], axis=0
            )
            scores = [
                lax.dot_general(
                    qk[:, column + LANES : column + 2 * LANES], queries, NT,
                    preferred_element_type=jnp.float32,
                )
                for qk, _ in parts
            ]
            largest = jnp.maximum(*[jnp.max(part, axis=0, keepdims=True) for part in scores])
            mixed = sum(
                jnp.dot(
                    vt[HP * head : HP * head + HP],
                    jnp.exp2((part - largest) * EXP2_SCALE).astype(jnp.bfloat16),
                    preferred_element_type=jnp.float32,
                )
                for part, (_, vt) in zip(scores, parts)
            )
            outs.append(mixed[:HD] / mixed[HD : HD + 1])
        both = jnp.concatenate(outs, axis=0).astype(jnp.bfloat16)
        for part in range(2):
            out_ref[place_ref[2 * number + part]] = both[:, part * LANES : (part + 1) * LANES]


def middle_kernel(mixed_ref, tables_ref, tokens_ref, modulation_ref, out_ref, table_ref, sem):
    copy = pltpu.make_async_copy(tables_ref.at[pl.ds(0, 9), :, pl.ds(LANES, 64), :], table_ref, sem)
    copy.start()
    slots = [mixed_ref[2 * zh + core] for core in range(2) for zh in range(4)]
    mixed = jnp.concatenate(
        [slot[16 * number : 16 * number + 16] for number in range(9) for slot in slots], axis=0
    )
    copy.wait()
    table = table_ref[...].reshape(-1, table_ref.shape[-1])
    branch = lax.dot_general(mixed, table, TN, preferred_element_type=jnp.float32)
    out_ref[...] = (
        tokens_ref[...].astype(jnp.float32) + modulation_ref[0, 2:3] * branch
    ).astype(jnp.bfloat16)


def time_kernel(
    positions, place_ref, middle_ref, tables_ref, out_table_ref, modulation_ref, out_ref,
    input_ref, mixed_ref, table_ref, sem,
):
    step = pl.program_id(0)
    copy = pltpu.make_async_copy(out_table_ref, table_ref, sem)

    @pl.when(step == 0)
    def _():
        copy.start()
        input_ref[...] = modulated(
            middle_ref[...].astype(jnp.float32), modulation_ref[1, 0:1], modulation_ref[1, 1:2]
        )

    rows, width = input_ref.shape
    one = lax.broadcasted_iota(jnp.int32, (rows, rows), 0) % positions
    two = lax.broadcasted_iota(jnp.int32, (rows, rows), 1) % positions
    same = one == two
    triples = []
    for slot in range(4):
        table = tables_ref[0, 0:7, 32 * slot : 32 * slot + 32].reshape(7 * 32, width)
        triples.append(lax.dot_general(table, input_ref[...], NT, preferred_element_type=jnp.float32))
    scores = []
    for triple in triples:
        queries = triple[:HD].astype(jnp.bfloat16)
        keys = triple[HD : 2 * HD].astype(jnp.bfloat16)
        part = lax.dot_general(keys, queries, TN, preferred_element_type=jnp.float32)
        scores.append(jnp.where(same, part, -1e30))
    raised = [
        jnp.exp2((part - jnp.max(part, axis=0, keepdims=True)) * EXP2_SCALE) for part in scores
    ]
    for slot in range(4):
        values = jnp.concatenate([triples[slot][2 * HD : 192], triples[slot][200:]], axis=0)
        total = jnp.sum(raised[slot], axis=0, keepdims=True)
        mixed = jnp.dot(
            values.astype(jnp.bfloat16), raised[slot].astype(jnp.bfloat16),
            preferred_element_type=jnp.float32,
        )
        mixed_ref[step * 4 + (place_ref[8] + 4 - slot) % 4] = mixed / total

    @pl.when(step == pl.num_programs(0) - 1)
    def _():
        copy.wait()
        mixed = mixed_ref[...].reshape(-1, rows).astype(jnp.bfloat16)
        branch = lax.dot_general(mixed, table_ref[...], TN, preferred_element_type=jnp.float32)
        out_ref[...] = (
            middle_ref[...].astype(jnp.float32) + modulation_ref[1, 2:3] * branch
        ).astype(jnp.bfloat16)


def rotation(count, by):
    return [(index, (index + by) % count) for index in range(count)]


SWAP = [(0, 1), (1, 0)]


def shards(tokens, frame_qkv, frame_out, time_qkv, time_out, modulation):
    tokens = tokens[0]
    rows, width = tokens.shape
    half = rows // 2
    zh, core = lax.axis_index("zh"), lax.axis_index("c")

    def along(array, axis, by):
        return lax.ppermute(array, axis, rotation(4, by))

    def swapped(array):
        return lax.ppermute(array, "c", SWAP)

    before, after = along(tokens, "zh", 1), along(tokens, "zh", 3)
    beside = swapped(tokens)
    far_top, far_bottom = along(before[:half], "zh", 1), along(after[half:], "zh", 3)
    early = [tokens, beside, before, after]
    late = [swapped(before), swapped(after), far_top, far_bottom, swapped(far_top), swapped(far_bottom)]
    spots = [zh, (zh + 3) % 4, (zh + 1) % 4, (zh + 2) % 4]
    place = [spot * 2 + side for spot in spots for side in (core, 1 - core)]
    place = jnp.stack(place + [lax.axis_index("zl")]).astype(jnp.int32)

    x, y, zl = lax.axis_index("x"), lax.axis_index("y"), lax.axis_index("zl")
    time_part = lax.dynamic_slice_in_dim(time_qkv, jnp.minimum(32 * (2 * y + core), 216 - 32), 32, 0)
    out_part = lax.dynamic_slice_in_dim(frame_out, 16 * jnp.minimum(4 * x + y, 8), 16, 0)
    time_parts = [time_part] + [along(time_part, "zl", by) for by in (1, 2, 3)]
    out_parts = lax.all_gather(out_part, "zh", axis=0, tiled=True)
    parts = jnp.concatenate(time_parts + [out_parts], axis=0)
    tables = lax.all_gather(parts, ("x", "y", "c"), axis=0)
    tables = tables.reshape(4, 8, 192, width)

    wqk, wvt = pl.pallas_call(
        spread_kernel,
        out_shape=(
            jax.ShapeDtypeStruct((4 * LANES, width), jnp.bfloat16),
            jax.ShapeDtypeStruct((2 * HP, width), jnp.bfloat16),
        ),
        in_specs=[whole()],
        out_specs=(whole(), whole()),
        compiler_params=params(),
        name="spread",
    )(frame_qkv.T)

    soon = rows * len(early)
    qk, vt = pl.pallas_call(
        early_kernel,
        out_shape=(
            jax.ShapeDtypeStruct((soon, 4 * LANES), jnp.bfloat16),
            jax.ShapeDtypeStruct((2 * HP, soon), jnp.bfloat16),
        ),
        in_specs=[whole()] * (len(early) + 3),
        out_specs=(whole(), whole()),
        compiler_params=params(),
        cost_estimate=pl.CostEstimate(flops=2 * 10**9, bytes_accessed=5 * 10**6, transcendentals=0),
        name="early_triples",
    )(*early, modulation, wqk, wvt)

    rest = 4 * rows
    mixed = pl.pallas_call(
        frame_kernel,
        out_shape=jax.ShapeDtypeStruct(((soon + rest) // LANES, 2 * HD, LANES), jnp.bfloat16),
        in_specs=[pl.BlockSpec(memory_space=pltpu.SMEM)] + [whole()] * 11,
        out_specs=whole(),
        scratch_shapes=[
            pltpu.VMEM((rest, 4 * LANES), jnp.bfloat16),
            pltpu.VMEM((2 * HP, rest), jnp.bfloat16),
        ],
        compiler_params=params(),
        name="frame_attention",
    )(place, *late, qk, vt, modulation, wqk, wvt)

    mixed = lax.all_to_all(mixed, ("zh", "c"), 0, 0, tiled=True)
    middle = pl.pallas_call(
        middle_kernel,
        out_shape=jax.ShapeDtypeStruct((rows, width), jnp.bfloat16),
        in_specs=[whole(), pl.BlockSpec(memory_space=pl.ANY), whole(), whole()],
        out_specs=whole(),
        scratch_shapes=[pltpu.VMEM((9, 2, 64, width), jnp.bfloat16), pltpu.SemaphoreType.DMA],
        compiler_params=params(),
        name="middle",
    )(mixed, tables.reshape(16, 2, 192, width), tokens, modulation)

    middle = lax.all_to_all(middle, ("x", "zl"), 0, 0, tiled=True)

    out = pl.pallas_call(
        functools.partial(time_kernel, rows // 16),
        grid=(4,),
        out_shape=jax.ShapeDtypeStruct((rows, width), jnp.bfloat16),
        in_specs=[
            pl.BlockSpec(memory_space=pltpu.SMEM),
            whole(),
            pl.BlockSpec((1, 8, LANES, width), lambda i: (i, 0, 0, 0)),
            pl.BlockSpec(memory_space=pl.ANY),
            whole(),
        ],
        out_specs=whole(),
        scratch_shapes=[
            pltpu.VMEM((rows, width), jnp.bfloat16),
            pltpu.VMEM((16, HD, rows), jnp.float32),
            pltpu.VMEM((width, width), jnp.bfloat16),
            pltpu.SemaphoreType.DMA,
        ],
        compiler_params=params(),
        name="time_block",
    )(place, middle, tables, time_out, modulation)
    out = lax.all_to_all(out, ("x", "zl"), 0, 0, tiled=True)
    return out[None]


def solution(mesh):
    fine = Mesh(mesh.devices.reshape(4, 4, 4, 4, 2), ("y", "x", "zl", "zh", "c"))
    frames, space = ("y", "x", "zl"), ("zh", "c")
    placed = (
        P(frames, space, None),
        P(None, space),
        P(space, None),
        P(("x", "zl"), None),
        P(),
        P("y", None, None),
    )
    return jax.shard_map(
        shards,
        mesh=fine,
        in_specs=placed,
        out_specs=P(frames, space, None),
        check_vma=False,
    )
```

```python
import functools
import math

import jax
import jax.numpy as jnp
from jax import lax
from jax.experimental import pallas as pl
from jax.experimental.pallas import tpu as pltpu
from jax.sharding import Mesh
from jax.sharding import PartitionSpec as P

HD = 72
HP = 80
LANES = 128
EPS = 1e-06
EXP2_SCALE = HD ** (-0.5) * math.log2(math.e)
NT = (((1,), (1,)), ((), ()))
TN = (((0,), (0,)), ((), ()))


def params(mib=28):
    return pltpu.CompilerParams(vmem_limit_bytes=mib * 1024 * 1024)


def whole():
    return pl.BlockSpec(memory_space=pltpu.VMEM)


def modulated(values, offset, stretch):
    center = jnp.mean(values, axis=-1, keepdims=True)
    values = values - center
    spread = jnp.mean(values * values, axis=-1, keepdims=True)
    return (values * lax.rsqrt(spread + EPS) * (1.0 + stretch) + offset).astype(jnp.bfloat16)


def triples_of(rows, modulation_ref, wqk_ref, wvt_ref):
    normed = modulated(rows, modulation_ref[0, 0:1], modulation_ref[0, 1:2])
    qk = lax.dot_general(normed, wqk_ref[...], NT, preferred_element_type=jnp.float32).astype(jnp.bfloat16)
    values = lax.dot_general(wvt_ref[...], normed, NT, preferred_element_type=jnp.float32)
    index = lax.broadcasted_iota(jnp.int32, values.shape, 0)
    ones = (index == HD) | (index == HP + HD)
    return qk, jnp.where(ones, 1.0, values).astype(jnp.bfloat16)


def spread_kernel(table_ref, wqk_ref, wvt_ref):
    table = table_ref[...].astype(jnp.float32)
    width = table.shape[1]
    wide, narrow = jnp.zeros((LANES - HD, width)), jnp.zeros((HP - HD, width))
    pieces = [table[HD * index : HD * index + HD] for index in range(6)]
    wqk_ref[...] = jnp.concatenate(
        [pieces[0], wide, pieces[1], wide, pieces[3], wide, pieces[4], wide], axis=0
    ).astype(jnp.bfloat16)
    wvt_ref[...] = jnp.concatenate([pieces[2], narrow, pieces[5], narrow], axis=0).astype(jnp.bfloat16)


def early_kernel(*refs):
    pieces, (modulation_ref, wqk_ref, wvt_ref, qk_ref, vt_ref) = refs[:-5], refs[-5:]
    for index in range(0, len(pieces), 2):
        rows = jnp.concatenate([pieces[index][:LANES], pieces[index + 1][:LANES]], axis=0)
        qk, vt = triples_of(rows.astype(jnp.float32), modulation_ref, wqk_ref, wvt_ref)
        start = LANES * index
        qk_ref[start : start + 2 * LANES] = qk
        vt_ref[:, start : start + 2 * LANES] = vt


def frame_kernel(
    place_ref, below_ref, above_ref, one_ref, two_ref, three_ref, four_ref, qk_ref, vt_ref, modulation_ref,
    wqk_ref, wvt_ref, out_ref, qk_late_ref, vt_late_ref,
):
    groups = ((below_ref, above_ref), (three_ref, four_ref, one_ref, two_ref))
    for index, group in enumerate(groups):
        rows = jnp.concatenate([ref[:LANES] for ref in group], axis=0).astype(jnp.float32)
        qk, vt = triples_of(rows, modulation_ref, wqk_ref, wvt_ref)
        start = 2 * LANES * index
        qk_late_ref[start : start + 2 * LANES] = qk
        vt_late_ref[:, start : start + 2 * LANES] = vt
    parts = ((qk_ref, vt_ref), (qk_late_ref, vt_late_ref))
    blocks = (
        ((qk_ref, 0), (qk_ref, 128)),
        ((qk_ref, 256), (qk_late_ref, 0)),
        ((qk_ref, 384), (qk_late_ref, 128)),
        ((qk_late_ref, 384), (qk_late_ref, 256)),
    )
    for number, block in enumerate(blocks):
        outs = []
        for head in range(2):
            column = 2 * LANES * head
            queries = jnp.concatenate(
                [ref[start : start + LANES, column : column + LANES] for ref, start in block], axis=0
            )
            scores = [
                lax.dot_general(
                    qk[:, column + LANES : column + 2 * LANES], queries, NT,
                    preferred_element_type=jnp.float32,
                )
                for qk, _ in parts
            ]
            largest = jnp.maximum(*[jnp.max(part, axis=0, keepdims=True) for part in scores])
            mixed = sum(
                jnp.dot(
                    vt[HP * head : HP * head + HP],
                    jnp.exp2((part - largest) * EXP2_SCALE).astype(jnp.bfloat16),
                    preferred_element_type=jnp.float32,
                )
                for part, (_, vt) in zip(scores, parts)
            )
            outs.append(mixed[:HD] / mixed[HD : HD + 1])
        both = jnp.concatenate(outs, axis=0).astype(jnp.bfloat16)
        for part in range(2):
            out_ref[place_ref[2 * number + part]] = both[:, part * LANES : (part + 1) * LANES]


def pack_kernel(times_ref, own_ref, below_ref, across_ref, above_ref, out_ref):
    count, rows = times_ref.shape[0], own_ref.shape[0]
    out_ref[:count] = times_ref[...]
    slots = (own_ref[...], below_ref[LANES:], across_ref[...], above_ref[LANES:])
    for index, slot in enumerate(slots):
        out_ref[count + rows * index : count + rows * index + rows] = slot


def join_kernel(mixed_ref, tokens_ref, out_ref):
    width = tokens_ref.shape[1]
    mixed = mixed_ref[...].reshape(-1, LANES).astype(jnp.float32)
    out_ref[:, :width] = mixed.T.astype(jnp.bfloat16)
    out_ref[:, width:] = tokens_ref[...]


def time_kernel(
    positions, place_ref, joined_ref, tables_ref, all_ref, out_table_ref, modulation_ref, out_ref,
    middle_ref, input_ref, mixed_ref, frame_table_ref, time_table_ref, frame_sem, time_sem,
):
    step = pl.program_id(0)
    rows, width = input_ref.shape
    zh = place_ref[8]
    time_copy = pltpu.make_async_copy(out_table_ref, time_table_ref, time_sem)

    @pl.when(step == 0)
    def _():
        frame_copies = [
            pltpu.make_async_copy(
                all_ref.at[pl.ds(0, 9), core, pl.ds(LANES + 16 * slot, 16), :],
                frame_table_ref.at[2 * ((zh + 4 - slot) % 4) + core],
                frame_sem.at[2 * slot + core],
            )
            for slot in range(4)
            for core in range(2)
        ]
        for copy in frame_copies:
            copy.start()
        time_copy.start()
        for copy in frame_copies:
            copy.wait()
        table = frame_table_ref[...].reshape(width, width)
        branch = jnp.dot(joined_ref[:, :width], table, preferred_element_type=jnp.float32)
        middle = joined_ref[:, width:].astype(jnp.float32) + modulation_ref[0, 2:3] * branch
        middle = middle.astype(jnp.bfloat16)
        middle_ref[...] = middle
        input_ref[...] = modulated(
            middle.astype(jnp.float32), modulation_ref[1, 0:1], modulation_ref[1, 1:2]
        )

    @pl.when(step > 0)
    def _():
        one = lax.broadcasted_iota(jnp.int32, (rows, rows), 0) % positions
        two = lax.broadcasted_iota(jnp.int32, (rows, rows), 1) % positions
        same = one == two
        triples = []
        for head in range(4):
            table = tables_ref[0, 0:7, 32 * head : 32 * head + 32].reshape(7 * 32, width)
            triples.append(
                lax.dot_general(table, input_ref[...], NT, preferred_element_type=jnp.float32)
            )
        scores = []
        for triple in triples:
            queries = triple[:HD].astype(jnp.bfloat16)
            keys = triple[HD : 2 * HD].astype(jnp.bfloat16)
            part = lax.dot_general(keys, queries, TN, preferred_element_type=jnp.float32)
            scores.append(jnp.where(same, part, -1e30))
        raised = [
            jnp.exp2((part - jnp.max(part, axis=0, keepdims=True)) * EXP2_SCALE) for part in scores
        ]
        for head in range(4):
            values = jnp.concatenate([triples[head][2 * HD : 192], triples[head][200:]], axis=0)
            total = jnp.sum(raised[head], axis=0, keepdims=True)
            mixed = jnp.dot(
                values.astype(jnp.bfloat16), raised[head].astype(jnp.bfloat16),
                preferred_element_type=jnp.float32,
            )
            mixed_ref[(step - 1) * 4 + head] = mixed / total

    @pl.when(step == pl.num_programs(0) - 1)
    def _():
        time_copy.wait()
        mixed = mixed_ref[...].reshape(-1, rows).astype(jnp.bfloat16)
        branch = lax.dot_general(mixed, time_table_ref[...], TN, preferred_element_type=jnp.float32)
        out_ref[...] = (
            middle_ref[...].astype(jnp.float32) + modulation_ref[1, 2:3] * branch
        ).astype(jnp.bfloat16)


def rotation(count, by):
    return [(index, (index + by) % count) for index in range(count)]


SWAP = [(0, 1), (1, 0)]


def shards(tokens, frame_qkv, frame_out, time_qkv, time_out, modulation):
    tokens = tokens[0]
    rows, width = tokens.shape
    half = rows // 2
    zh, core = lax.axis_index("zh"), lax.axis_index("c")

    def along(array, axis, by):
        return lax.ppermute(array, axis, rotation(4, by))

    def swapped(array):
        return lax.ppermute(array, "c", SWAP)

    x, y = lax.axis_index("x"), lax.axis_index("y")
    time_part = lax.dynamic_slice_in_dim(time_qkv, jnp.minimum(32 * (2 * y + core), 216 - 32), 32, 0)
    out_part = lax.dynamic_slice_in_dim(frame_out, 16 * jnp.minimum(4 * x + y, 8), 16, 0)
    across = along(out_part, "zh", 2)

    sent = jnp.concatenate([tokens, out_part], axis=0)
    before, after = along(sent, "zh", 1), along(sent, "zh", 3)
    beside = swapped(tokens)
    times = lax.all_gather(time_part, "zl", axis=0, tiled=True)
    parts = pl.pallas_call(
        pack_kernel,
        out_shape=jax.ShapeDtypeStruct((4 * 32 + 4 * 16, width), times.dtype),
        in_specs=[whole()] * 5,
        out_specs=whole(),
        compiler_params=params(),
        name="pack",
    )(times, out_part, before, across, after)
    tables = lax.all_gather(parts, ("x", "y", "c"), axis=0)
    far_top, far_bottom = along(before[:half], "zh", 1), along(after[half:rows], "zh", 3)
    early = [tokens, beside, before, after]
    late = [swapped(before), swapped(after), far_top, far_bottom, swapped(far_top), swapped(far_bottom)]
    spots = [zh, (zh + 3) % 4, (zh + 1) % 4, (zh + 2) % 4]
    place = [spot * 2 + side for spot in spots for side in (core, 1 - core)]
    place = jnp.stack(place + [zh]).astype(jnp.int32)

    tables = tables.reshape(4, 8, 192, width)

    wqk, wvt = pl.pallas_call(
        spread_kernel,
        out_shape=(
            jax.ShapeDtypeStruct((4 * LANES, width), jnp.bfloat16),
            jax.ShapeDtypeStruct((2 * HP, width), jnp.bfloat16),
        ),
        in_specs=[whole()],
        out_specs=(whole(), whole()),
        compiler_params=params(),
        name="spread",
    )(frame_qkv.T)

    soon = rows * len(early)
    qk, vt = pl.pallas_call(
        early_kernel,
        out_shape=(
            jax.ShapeDtypeStruct((soon, 4 * LANES), jnp.bfloat16),
            jax.ShapeDtypeStruct((2 * HP, soon), jnp.bfloat16),
        ),
        in_specs=[whole()] * (len(early) + 3),
        out_specs=(whole(), whole()),
        compiler_params=params(),
        cost_estimate=pl.CostEstimate(flops=2 * 10**9, bytes_accessed=5 * 10**6, transcendentals=0),
        name="early_triples",
    )(*early, modulation, wqk, wvt)

    rest = 4 * rows
    mixed = pl.pallas_call(
        frame_kernel,
        out_shape=jax.ShapeDtypeStruct(((soon + rest) // LANES, 2 * HD, LANES), jnp.bfloat16),
        in_specs=[pl.BlockSpec(memory_space=pltpu.SMEM)] + [whole()] * 11,
        out_specs=whole(),
        scratch_shapes=[
            pltpu.VMEM((rest, 4 * LANES), jnp.bfloat16),
            pltpu.VMEM((2 * HP, rest), jnp.bfloat16),
        ],
        compiler_params=params(),
        name="frame_attention",
    )(place, *late, qk, vt, modulation, wqk, wvt)

    mixed = lax.all_to_all(mixed, ("zh", "c"), 0, 0, tiled=True)
    joined = pl.pallas_call(
        join_kernel,
        out_shape=jax.ShapeDtypeStruct((rows, 2 * width), jnp.bfloat16),
        in_specs=[whole(), whole()],
        out_specs=whole(),
        compiler_params=params(),
        name="join",
    )(mixed, tokens)
    joined = lax.all_to_all(joined, ("x", "zl"), 0, 0, tiled=True)

    out = pl.pallas_call(
        functools.partial(time_kernel, rows // 16),
        grid=(5,),
        out_shape=jax.ShapeDtypeStruct((rows, width), jnp.bfloat16),
        in_specs=[
            pl.BlockSpec(memory_space=pltpu.SMEM),
            whole(),
            pl.BlockSpec((1, 8, LANES, width), lambda i: (jnp.maximum(i - 1, 0), 0, 0, 0)),
            pl.BlockSpec(memory_space=pl.ANY),
            pl.BlockSpec(memory_space=pl.ANY),
            whole(),
        ],
        out_specs=whole(),
        scratch_shapes=[
            pltpu.VMEM((rows, width), jnp.bfloat16),
            pltpu.VMEM((rows, width), jnp.bfloat16),
            pltpu.VMEM((16, HD, rows), jnp.float32),
            pltpu.VMEM((8, 9, 16, width), jnp.bfloat16),
            pltpu.VMEM((width, width), jnp.bfloat16),
            pltpu.SemaphoreType.DMA((8,)),
            pltpu.SemaphoreType.DMA,
        ],
        compiler_params=params(56),
        name="time_block",
    )(place, joined, tables, tables.reshape(16, 2, 192, width), time_out, modulation)
    out = lax.all_to_all(out, ("x", "zl"), 0, 0, tiled=True)
    return out[None]


def solution(mesh):
    fine = Mesh(mesh.devices.reshape(4, 4, 4, 4, 2), ("y", "x", "zl", "zh", "c"))
    frames, space = ("y", "x", "zl"), ("zh", "c")
    placed = (
        P(frames, space, None),
        P(None, space),
        P(space, None),
        P(("x", "zl"), None),
        P(),
        P("y", None, None),
    )
    return jax.shard_map(
        shards,
        mesh=fine,
        in_specs=placed,
        out_specs=P(frames, space, None),
        check_vma=False,
    )
```

```python
import functools
import math

import jax
import jax.numpy as jnp
from jax import lax
from jax.experimental import pallas as pl
from jax.experimental.pallas import tpu as pltpu
from jax.sharding import Mesh
from jax.sharding import PartitionSpec as P

HD = 72
HP = 80
LANES = 128
EPS = 1e-06
EXP2_SCALE = HD ** (-0.5) * math.log2(math.e)
NT = (((1,), (1,)), ((), ()))
TN = (((0,), (0,)), ((), ()))


def params(mib=48):
    return pltpu.CompilerParams(vmem_limit_bytes=mib * 1024 * 1024)


def whole():
    return pl.BlockSpec(memory_space=pltpu.VMEM)


def modulated(values, offset, stretch):
    center = jnp.mean(values, axis=-1, keepdims=True)
    values = values - center
    spread = jnp.mean(values * values, axis=-1, keepdims=True)
    return (values * lax.rsqrt(spread + EPS) * (1.0 + stretch) + offset).astype(jnp.bfloat16)


def triples_of(rows, modulation_ref, wqk_ref, wvt_ref):
    normed = modulated(rows, modulation_ref[0, 0:1], modulation_ref[0, 1:2])
    qk = lax.dot_general(normed, wqk_ref[...], NT, preferred_element_type=jnp.float32).astype(jnp.bfloat16)
    values = lax.dot_general(wvt_ref[...], normed, NT, preferred_element_type=jnp.float32)
    index = lax.broadcasted_iota(jnp.int32, values.shape, 0)
    ones = (index == HD) | (index == HP + HD)
    return qk, jnp.where(ones, 1.0, values).astype(jnp.bfloat16)


def spread_kernel(table_ref, wqk_ref, wvt_ref):
    table = table_ref[...].astype(jnp.float32)
    width = table.shape[1]
    wide, narrow = jnp.zeros((LANES - HD, width)), jnp.zeros((HP - HD, width))
    pieces = [table[HD * index : HD * index + HD] for index in range(6)]
    wqk_ref[...] = jnp.concatenate(
        [pieces[0], wide, pieces[1], wide, pieces[3], wide, pieces[4], wide], axis=0
    ).astype(jnp.bfloat16)
    wvt_ref[...] = jnp.concatenate([pieces[2], narrow, pieces[5], narrow], axis=0).astype(jnp.bfloat16)


def early_kernel(*refs):
    pieces, (modulation_ref, wqk_ref, wvt_ref, qk_ref, vt_ref) = refs[:-5], refs[-5:]
    for index in range(0, len(pieces), 2):
        rows = jnp.concatenate([pieces[index][...], pieces[index + 1][...]], axis=0)
        qk, vt = triples_of(rows.astype(jnp.float32), modulation_ref, wqk_ref, wvt_ref)
        start = LANES * index
        qk_ref[start : start + 2 * LANES] = qk
        vt_ref[:, start : start + 2 * LANES] = vt


def frame_kernel(
    place_ref, below_ref, above_ref, one_ref, two_ref, three_ref, four_ref, qk_ref, vt_ref, modulation_ref,
    wqk_ref, wvt_ref, out_ref, qk_late_ref, vt_late_ref,
):
    groups = ((below_ref, above_ref), (three_ref, four_ref, one_ref, two_ref))
    for index, group in enumerate(groups):
        rows = jnp.concatenate([ref[...] for ref in group], axis=0).astype(jnp.float32)
        qk, vt = triples_of(rows, modulation_ref, wqk_ref, wvt_ref)
        start = 2 * LANES * index
        qk_late_ref[start : start + 2 * LANES] = qk
        vt_late_ref[:, start : start + 2 * LANES] = vt
    parts = ((qk_ref, vt_ref), (qk_late_ref, vt_late_ref))
    blocks = (
        ((qk_ref, 0), (qk_ref, 128)),
        ((qk_ref, 256), (qk_late_ref, 0)),
        ((qk_ref, 384), (qk_late_ref, 128)),
        ((qk_late_ref, 384), (qk_late_ref, 256)),
    )
    for number, block in enumerate(blocks):
        outs = []
        for head in range(2):
            column = 2 * LANES * head
            queries = jnp.concatenate(
                [ref[start : start + LANES, column : column + LANES] for ref, start in block], axis=0
            )
            scores = [
                lax.dot_general(
                    qk[:, column + LANES : column + 2 * LANES], queries, NT,
                    preferred_element_type=jnp.float32,
                )
                for qk, _ in parts
            ]
            largest = jnp.maximum(*[jnp.max(part, axis=0, keepdims=True) for part in scores])
            mixed = sum(
                jnp.dot(
                    vt[HP * head : HP * head + HP],
                    jnp.exp2((part - largest) * EXP2_SCALE).astype(jnp.bfloat16),
                    preferred_element_type=jnp.float32,
                )
                for part, (_, vt) in zip(scores, parts)
            )
            outs.append(mixed[:HD] / mixed[HD : HD + 1])
        both = jnp.concatenate(outs, axis=0).astype(jnp.bfloat16)
        for part in range(2):
            out_ref[place_ref[2 * number + part]] = both[:, part * LANES : (part + 1) * LANES]


def pack_kernel(parts_ref, out_ref):
    parts = parts_ref[...].astype(jnp.float32)
    rows = [parts[16 * (4 * zh + zl) : 16 * (4 * zh + zl) + 8] for zl in range(4) for zh in range(4)]
    rows += [parts[16 * (4 * zh + zl) + 8 : 16 * (4 * zh + zl) + 16] for zh in range(4) for zl in range(2)]
    out_ref[...] = jnp.concatenate(rows, axis=0).astype(jnp.bfloat16)


def middle_kernel(mixed_ref, tables_ref, tokens_ref, modulation_ref, out_ref, table_ref, sem):
    copy = pltpu.make_async_copy(tables_ref.at[pl.ds(0, 9), :, pl.ds(LANES, 64), :], table_ref, sem)
    copy.start()
    slots = [mixed_ref[2 * zh + core] for core in range(2) for zh in range(4)]
    mixed = jnp.concatenate(
        [slot[16 * number : 16 * number + 16] for number in range(9) for slot in slots], axis=0
    )
    copy.wait()
    table = table_ref[...].reshape(-1, table_ref.shape[-1])
    branch = lax.dot_general(mixed, table, TN, preferred_element_type=jnp.float32)
    out_ref[...] = (
        tokens_ref[...].astype(jnp.float32) + modulation_ref[0, 2:3] * branch
    ).astype(jnp.bfloat16)


def time_attention(positions, triples, mixed_ref, first):
    rows = triples.shape[1]
    one = lax.broadcasted_iota(jnp.int32, (rows, rows), 0) % positions
    two = lax.broadcasted_iota(jnp.int32, (rows, rows), 1) % positions
    same = one == two
    scores, values = [], []
    for head in range(4):
        triple = jnp.concatenate(
            [triples[LANES * part + 32 * head : LANES * part + 32 * head + 32] for part in range(7)], axis=0
        )
        queries = triple[:HD].astype(jnp.bfloat16)
        keys = triple[HD : 2 * HD].astype(jnp.bfloat16)
        values.append(jnp.concatenate([triple[2 * HD : 192], triple[200:]], axis=0).astype(jnp.bfloat16))
        part = lax.dot_general(keys, queries, TN, preferred_element_type=jnp.float32)
        scores.append(jnp.where(same, part, -1e30))
    raised = [
        jnp.exp2((part - jnp.max(part, axis=0, keepdims=True)) * EXP2_SCALE) for part in scores
    ]
    for head in range(4):
        total = jnp.sum(raised[head], axis=0, keepdims=True)
        mixed = jnp.dot(values[head], raised[head].astype(jnp.bfloat16), preferred_element_type=jnp.float32)
        mixed_ref[first + head] = mixed / total


def time_kernel(
    positions, middle_ref, tables_ref, out_table_ref, modulation_ref, out_ref, mixed_ref,
):
    rows, width = middle_ref.shape
    second = modulated(
        middle_ref[...].astype(jnp.float32), modulation_ref[1, 0:1], modulation_ref[1, 1:2]
    )
    for group in range(4):
        table = tables_ref[group, 0:7, 0:LANES].reshape(7 * LANES, width)
        triples = lax.dot_general(table, second, NT, preferred_element_type=jnp.float32)
        time_attention(positions, triples, mixed_ref, 4 * group)
    mixed = mixed_ref[...].reshape(-1, rows).astype(jnp.bfloat16)
    branch = lax.dot_general(mixed, out_table_ref[...], TN, preferred_element_type=jnp.float32)
    out_ref[...] = (
        middle_ref[...].astype(jnp.float32) + modulation_ref[1, 2:3] * branch
    ).astype(jnp.bfloat16)


def rotation(count, by):
    return [(index, (index + by) % count) for index in range(count)]


SWAP = [(0, 1), (1, 0)]


def shards(tokens, frame_qkv, frame_out, time_qkv, time_out, modulation):
    tokens = tokens[0]
    rows, width = tokens.shape
    half = rows // 2
    zh, core = lax.axis_index("zh"), lax.axis_index("c")

    def along(array, axis, by):
        return lax.ppermute(array, axis, rotation(4, by))

    def swapped(array):
        return lax.ppermute(array, "c", SWAP)

    before, after = along(tokens, "zh", 1), along(tokens, "zh", 3)
    beside = swapped(tokens)
    far_top, far_bottom = along(before[:half], "zh", 1), along(after[half:], "zh", 3)
    early = [tokens, beside, before, after]
    late = [swapped(before), swapped(after), far_top, far_bottom, swapped(far_top), swapped(far_bottom)]
    spots = [zh, (zh + 3) % 4, (zh + 1) % 4, (zh + 2) % 4]
    place = jnp.stack(
        [spot * 2 + side for spot in spots for side in (core, 1 - core)]
    ).astype(jnp.int32)

    x, y, zl = lax.axis_index("x"), lax.axis_index("y"), lax.axis_index("zl")
    start = jnp.minimum(32 * (2 * y + core), 216 - 32) + 8 * zh
    time_part = lax.dynamic_slice_in_dim(time_qkv, start, 8, 0)
    start = 16 * jnp.minimum(4 * x + y, 8) + 8 * (zl % 2)
    out_part = lax.dynamic_slice_in_dim(frame_out, start, 8, 0)
    part = jnp.concatenate([time_part, out_part], axis=0)
    parts = lax.all_gather(part, ("zh", "zl"), axis=0, tiled=True)
    parts = pl.pallas_call(
        pack_kernel,
        out_shape=jax.ShapeDtypeStruct((4 * 32 + 4 * 16, width), parts.dtype),
        in_specs=[whole()],
        out_specs=whole(),
        compiler_params=params(),
        name="pack",
    )(parts)
    tables = lax.all_gather(parts, ("x", "y", "c"), axis=0)
    tables = tables.reshape(4, 8, 192, width)

    wqk, wvt = pl.pallas_call(
        spread_kernel,
        out_shape=(
            jax.ShapeDtypeStruct((4 * LANES, width), jnp.bfloat16),
            jax.ShapeDtypeStruct((2 * HP, width), jnp.bfloat16),
        ),
        in_specs=[whole()],
        out_specs=(whole(), whole()),
        compiler_params=params(),
        name="spread",
    )(frame_qkv.T)

    soon = rows * len(early)
    qk, vt = pl.pallas_call(
        early_kernel,
        out_shape=(
            jax.ShapeDtypeStruct((soon, 4 * LANES), jnp.bfloat16),
            jax.ShapeDtypeStruct((2 * HP, soon), jnp.bfloat16),
        ),
        in_specs=[whole()] * (len(early) + 3),
        out_specs=(whole(), whole()),
        compiler_params=params(),
        cost_estimate=pl.CostEstimate(flops=2 * 10**9, bytes_accessed=5 * 10**6, transcendentals=0),
        name="early_triples",
    )(*early, modulation, wqk, wvt)

    rest = 4 * rows
    mixed = pl.pallas_call(
        frame_kernel,
        out_shape=jax.ShapeDtypeStruct(((soon + rest) // LANES, 2 * HD, LANES), jnp.bfloat16),
        in_specs=[pl.BlockSpec(memory_space=pltpu.SMEM)] + [whole()] * 11,
        out_specs=whole(),
        scratch_shapes=[
            pltpu.VMEM((rest, 4 * LANES), jnp.bfloat16),
            pltpu.VMEM((2 * HP, rest), jnp.bfloat16),
        ],
        compiler_params=params(),
        name="frame_attention",
    )(place, *late, qk, vt, modulation, wqk, wvt)

    mixed = lax.all_to_all(mixed, ("zh", "c"), 0, 0, tiled=True)
    middle = pl.pallas_call(
        middle_kernel,
        out_shape=jax.ShapeDtypeStruct((rows, width), jnp.bfloat16),
        in_specs=[whole(), pl.BlockSpec(memory_space=pl.ANY), whole(), whole()],
        out_specs=whole(),
        scratch_shapes=[pltpu.VMEM((9, 2, 64, width), jnp.bfloat16), pltpu.SemaphoreType.DMA],
        compiler_params=params(44),
        name="middle",
    )(mixed, tables.reshape(16, 2, 192, width), tokens, modulation)

    middle = lax.all_to_all(middle, ("x", "zl"), 0, 0, tiled=True)

    out = pl.pallas_call(
        functools.partial(time_kernel, rows // 16),
        out_shape=jax.ShapeDtypeStruct((rows, width), jnp.bfloat16),
        in_specs=[whole()] * 4,
        out_specs=whole(),
        scratch_shapes=[pltpu.VMEM((16, HD, rows), jnp.float32)],
        compiler_params=params(28),
        name="time_block",
    )(middle, tables, time_out, modulation)
    out = lax.all_to_all(out, ("x", "zl"), 0, 0, tiled=True)
    return out[None]


def solution(mesh):
    fine = Mesh(mesh.devices.reshape(4, 4, 4, 4, 2), ("y", "x", "zl", "zh", "c"))
    frames, space = ("y", "x", "zl"), ("zh", "c")
    placed = (
        P(frames, space, None),
        P(None, space),
        P(space, None),
        P(("x", "zl"), None),
        P(),
        P("y", None, None),
    )
    return jax.shard_map(
        shards,
        mesh=fine,
        in_specs=placed,
        out_specs=P(frames, space, None),
        check_vma=False,
    )
```

```python
import functools
import math

import jax
import jax.numpy as jnp
from jax import lax
from jax.experimental import pallas as pl
from jax.experimental.pallas import tpu as pltpu
from jax.sharding import Mesh
from jax.sharding import PartitionSpec as P

HD = 72
HP = 80
LANES = 128
EPS = 1e-06
EXP2_SCALE = HD ** (-0.5) * math.log2(math.e)
NT = (((1,), (1,)), ((), ()))
TN = (((0,), (0,)), ((), ()))


def params(mib=16):
    return pltpu.CompilerParams(vmem_limit_bytes=mib * 1024 * 1024)


def whole():
    return pl.BlockSpec(memory_space=pltpu.VMEM)


def modulated(values, offset, stretch):
    center = jnp.mean(values, axis=-1, keepdims=True)
    values = values - center
    spread = jnp.mean(values * values, axis=-1, keepdims=True)
    return (values * lax.rsqrt(spread + EPS) * (1.0 + stretch) + offset).astype(jnp.bfloat16)


def triples_of(rows, modulation_ref, wqk_ref, wvt_ref):
    normed = modulated(rows, modulation_ref[0, 0:1], modulation_ref[0, 1:2])
    qk = lax.dot_general(normed, wqk_ref[...], NT, preferred_element_type=jnp.float32).astype(jnp.bfloat16)
    values = lax.dot_general(wvt_ref[...], normed, NT, preferred_element_type=jnp.float32)
    index = lax.broadcasted_iota(jnp.int32, values.shape, 0)
    ones = (index == HD) | (index == HP + HD)
    return qk, jnp.where(ones, 1.0, values).astype(jnp.bfloat16)


def spread_kernel(table_ref, wqk_ref, wvt_ref):
    table = table_ref[...].astype(jnp.float32)
    width = table.shape[1]
    wide, narrow = jnp.zeros((LANES - HD, width)), jnp.zeros((HP - HD, width))
    pieces = [table[HD * index : HD * index + HD] for index in range(6)]
    wqk_ref[...] = jnp.concatenate(
        [pieces[0], wide, pieces[1], wide, pieces[3], wide, pieces[4], wide], axis=0
    ).astype(jnp.bfloat16)
    wvt_ref[...] = jnp.concatenate([pieces[2], narrow, pieces[5], narrow], axis=0).astype(jnp.bfloat16)


def frame_kernel(*refs):
    place_ref, pieces = refs[0], refs[1:11]
    modulation_in, wqk_in, wvt_in, out_ref = refs[11:15]
    rows_ref, modulation_ref, wqk_ref, wvt_ref, qk_ref, vt_ref, sems = refs[15:]
    copies, start = [], 0
    for index, piece in enumerate(pieces):
        count = piece.shape[0]
        copies.append(pltpu.make_async_copy(piece, rows_ref.at[pl.ds(start, count)], sems.at[index]))
        start += count
    tables = [
        pltpu.make_async_copy(modulation_in, modulation_ref, sems.at[10]),
        pltpu.make_async_copy(wqk_in, wqk_ref, sems.at[11]),
        pltpu.make_async_copy(wvt_in, wvt_ref, sems.at[12]),
    ]
    for copy in copies[:2] + tables + copies[2:]:
        copy.start()
    block = 2 * LANES
    groups = (copies[0:2] + tables, copies[2:4], copies[4:6], copies[6:10])
    for index, group in enumerate(groups):
        for copy in group:
            copy.wait()
        start = block * index
        rows = rows_ref[start : start + block].astype(jnp.float32)
        qk, vt = triples_of(rows, modulation_ref, wqk_ref, wvt_ref)
        qk_ref[start : start + block] = qk
        vt_ref[:, start : start + block] = vt
    for index in range(len(groups)):
        start = block * index
        outs = []
        for head in range(2):
            column = 2 * LANES * head
            queries = qk_ref[start : start + block, column : column + LANES]
            keys = qk_ref[:, column + LANES : column + 2 * LANES]
            scores = lax.dot_general(keys, queries, NT, preferred_element_type=jnp.float32)
            largest = jnp.max(scores, axis=0, keepdims=True)
            raised = jnp.exp2((scores - largest) * EXP2_SCALE).astype(jnp.bfloat16)
            mixed = jnp.dot(
                vt_ref[HP * head : HP * head + HP], raised, preferred_element_type=jnp.float32
            )
            outs.append(mixed[:HD] / mixed[HD : HD + 1])
        both = jnp.concatenate(outs, axis=0).astype(jnp.bfloat16)
        for part in range(2):
            out_ref[place_ref[2 * index + part]] = both[:, part * LANES : (part + 1) * LANES]


def pack_kernel(parts_ref, out_ref):
    parts = parts_ref[...].astype(jnp.float32)
    rows = [parts[16 * (4 * zh + zl) : 16 * (4 * zh + zl) + 8] for zl in range(4) for zh in range(4)]
    rows += [parts[16 * (4 * zh + zl) + 8 : 16 * (4 * zh + zl) + 16] for zh in range(4) for zl in range(2)]
    out_ref[...] = jnp.concatenate(rows, axis=0).astype(jnp.bfloat16)


def middle_kernel(
    mixed_ref, tables_ref, tokens_ref, modulation_ref, out_ref, table_ref, held_ref, table_sem, held_sem
):
    copy = pltpu.make_async_copy(tables_ref.at[pl.ds(0, 9), :, pl.ds(LANES, 64), :], table_ref, table_sem)
    held_copy = pltpu.make_async_copy(tokens_ref, held_ref, held_sem)
    copy.start()
    held_copy.start()
    slots = [mixed_ref[2 * zh + core] for core in range(2) for zh in range(4)]
    mixed = jnp.concatenate(
        [slot[16 * number : 16 * number + 16] for number in range(9) for slot in slots], axis=0
    )
    copy.wait()
    held_copy.wait()
    table = table_ref[...].reshape(-1, table_ref.shape[-1])
    branch = lax.dot_general(mixed, table, TN, preferred_element_type=jnp.float32)
    out_ref[...] = (
        held_ref[...].astype(jnp.float32) + modulation_ref[0, 2:3] * branch
    ).astype(jnp.bfloat16)


def time_attention(positions, triples, mixed_ref, first):
    rows = triples.shape[1]
    one = lax.broadcasted_iota(jnp.int32, (rows, rows), 0) % positions
    two = lax.broadcasted_iota(jnp.int32, (rows, rows), 1) % positions
    same = one == two
    scores, values = [], []
    for head in range(4):
        triple = jnp.concatenate(
            [triples[LANES * part + 32 * head : LANES * part + 32 * head + 32] for part in range(7)], axis=0
        )
        queries = triple[:HD].astype(jnp.bfloat16)
        keys = triple[HD : 2 * HD].astype(jnp.bfloat16)
        values.append(jnp.concatenate([triple[2 * HD : 192], triple[200:]], axis=0).astype(jnp.bfloat16))
        part = lax.dot_general(keys, queries, TN, preferred_element_type=jnp.float32)
        scores.append(jnp.where(same, part, -1e30))
    raised = [
        jnp.exp2((part - jnp.max(part, axis=0, keepdims=True)) * EXP2_SCALE) for part in scores
    ]
    for head in range(4):
        total = jnp.sum(raised[head], axis=0, keepdims=True)
        mixed = jnp.dot(values[head], raised[head].astype(jnp.bfloat16), preferred_element_type=jnp.float32)
        mixed_ref[first + head] = mixed / total


def time_kernel(
    positions, middle_ref, tables_ref, out_table_ref, modulation_ref, out_ref, mixed_ref,
):
    rows, width = middle_ref.shape
    second = modulated(
        middle_ref[...].astype(jnp.float32), modulation_ref[1, 0:1], modulation_ref[1, 1:2]
    )
    for group in range(4):
        table = tables_ref[group, 0:7, 0:LANES].reshape(7 * LANES, width)
        triples = lax.dot_general(table, second, NT, preferred_element_type=jnp.float32)
        time_attention(positions, triples, mixed_ref, 4 * group)
    mixed = mixed_ref[...].reshape(-1, rows).astype(jnp.bfloat16)
    branch = lax.dot_general(mixed, out_table_ref[...], TN, preferred_element_type=jnp.float32)
    out_ref[...] = (
        middle_ref[...].astype(jnp.float32) + modulation_ref[1, 2:3] * branch
    ).astype(jnp.bfloat16)


def rotation(count, by):
    return [(index, (index + by) % count) for index in range(count)]


SWAP = [(0, 1), (1, 0)]


def shards(tokens, frame_qkv, frame_out, time_qkv, time_out, modulation):
    tokens = tokens[0]
    rows, width = tokens.shape
    half = rows // 2
    zh, core = lax.axis_index("zh"), lax.axis_index("c")

    def along(array, axis, by):
        return lax.ppermute(array, axis, rotation(4, by))

    def swapped(array):
        return lax.ppermute(array, "c", SWAP)

    before, after = along(tokens, "zh", 1), along(tokens, "zh", 3)
    beside = swapped(tokens)
    far_top, far_bottom = along(before[:half], "zh", 1), along(after[half:], "zh", 3)
    pieces = [tokens, beside, before, swapped(before), after, swapped(after)]
    pieces += [far_top, far_bottom, swapped(far_top), swapped(far_bottom)]
    spots = [zh, (zh + 3) % 4, (zh + 1) % 4, (zh + 2) % 4]
    place = jnp.stack(
        [spot * 2 + side for spot in spots for side in (core, 1 - core)]
    ).astype(jnp.int32)

    x, y, zl = lax.axis_index("x"), lax.axis_index("y"), lax.axis_index("zl")
    start = jnp.minimum(32 * (2 * y + core), 216 - 32) + 8 * zh
    time_part = lax.dynamic_slice_in_dim(time_qkv, start, 8, 0)
    start = 16 * jnp.minimum(4 * x + y, 8) + 8 * (zl % 2)
    out_part = lax.dynamic_slice_in_dim(frame_out, start, 8, 0)
    part = jnp.concatenate([time_part, out_part], axis=0)
    parts = lax.all_gather(part, ("zh", "zl"), axis=0, tiled=True)
    parts = pl.pallas_call(
        pack_kernel,
        out_shape=jax.ShapeDtypeStruct((4 * 32 + 4 * 16, width), parts.dtype),
        in_specs=[whole()],
        out_specs=whole(),
        compiler_params=params(),
        name="pack",
    )(parts)
    tables = lax.all_gather(parts, ("x", "y", "c"), axis=0)
    tables = tables.reshape(4, 8, 192, width)

    wqk, wvt = pl.pallas_call(
        spread_kernel,
        out_shape=(
            jax.ShapeDtypeStruct((4 * LANES, width), jnp.bfloat16),
            jax.ShapeDtypeStruct((2 * HP, width), jnp.bfloat16),
        ),
        in_specs=[whole()],
        out_specs=(whole(), whole()),
        compiler_params=params(),
        name="spread",
    )(frame_qkv.T)

    count = 8 * rows
    mixed = pl.pallas_call(
        frame_kernel,
        out_shape=jax.ShapeDtypeStruct((count // LANES, 2 * HD, LANES), jnp.bfloat16),
        in_specs=[pl.BlockSpec(memory_space=pltpu.SMEM)] + [pl.BlockSpec(memory_space=pl.ANY)] * 13,
        out_specs=whole(),
        scratch_shapes=[
            pltpu.VMEM((count, width), jnp.bfloat16),
            pltpu.VMEM(modulation.shape, modulation.dtype),
            pltpu.VMEM(wqk.shape, wqk.dtype),
            pltpu.VMEM(wvt.shape, wvt.dtype),
            pltpu.VMEM((count, 4 * LANES), jnp.bfloat16),
            pltpu.VMEM((2 * HP, count), jnp.bfloat16),
            pltpu.SemaphoreType.DMA((13,)),
        ],
        compiler_params=params(60),
        name="frame_attention",
    )(place, *pieces, modulation, wqk, wvt)

    mixed = lax.all_to_all(mixed, ("zh", "c"), 0, 0, tiled=True)
    middle = pl.pallas_call(
        middle_kernel,
        out_shape=jax.ShapeDtypeStruct((rows, width), jnp.bfloat16),
        in_specs=[whole(), pl.BlockSpec(memory_space=pl.ANY), pl.BlockSpec(memory_space=pl.ANY), whole()],
        out_specs=whole(),
        scratch_shapes=[
            pltpu.VMEM((9, 2, 64, width), jnp.bfloat16),
            pltpu.VMEM((rows, width), jnp.bfloat16),
            pltpu.SemaphoreType.DMA,
            pltpu.SemaphoreType.DMA,
        ],
        compiler_params=params(44),
        name="middle",
    )(mixed, tables.reshape(16, 2, 192, width), tokens, modulation)

    middle = lax.all_to_all(middle, ("x", "zl"), 0, 0, tiled=True)

    out = pl.pallas_call(
        functools.partial(time_kernel, rows // 16),
        out_shape=jax.ShapeDtypeStruct((rows, width), jnp.bfloat16),
        in_specs=[whole()] * 4,
        out_specs=whole(),
        scratch_shapes=[pltpu.VMEM((16, HD, rows), jnp.float32)],
        compiler_params=params(28),
        name="time_block",
    )(middle, tables, time_out, modulation)
    out = lax.all_to_all(out, ("x", "zl"), 0, 0, tiled=True)
    return out[None]


def solution(mesh):
    fine = Mesh(mesh.devices.reshape(4, 4, 4, 4, 2), ("y", "x", "zl", "zh", "c"))
    frames, space = ("y", "x", "zl"), ("zh", "c")
    placed = (
        P(frames, space, None),
        P(None, space),
        P(space, None),
        P(("x", "zl"), None),
        P(),
        P("y", None, None),
    )
    return jax.shard_map(
        shards,
        mesh=fine,
        in_specs=placed,
        out_specs=P(frames, space, None),
        check_vma=False,
    )
```

```python
import functools
import math

import jax
import jax.numpy as jnp
from jax import lax
from jax.experimental import pallas as pl
from jax.experimental.pallas import tpu as pltpu
from jax.sharding import Mesh
from jax.sharding import PartitionSpec as P

HD = 72
HP = 80
LANES = 128
EPS = 1e-06
EXP2_SCALE = HD ** (-0.5) * math.log2(math.e)
NT = (((1,), (1,)), ((), ()))
TN = (((0,), (0,)), ((), ()))


def params(mib=48):
    return pltpu.CompilerParams(vmem_limit_bytes=mib * 1024 * 1024)


def whole():
    return pl.BlockSpec(memory_space=pltpu.VMEM)


def modulated(values, offset, stretch):
    center = jnp.mean(values, axis=-1, keepdims=True)
    values = values - center
    spread = jnp.mean(values * values, axis=-1, keepdims=True)
    return (values * lax.rsqrt(spread + EPS) * (1.0 + stretch) + offset).astype(jnp.bfloat16)


def triples_of(rows, modulation_ref, wqk_ref, wvt_ref):
    normed = modulated(rows, modulation_ref[0, 0:1], modulation_ref[0, 1:2])
    qk = lax.dot_general(normed, wqk_ref[...], NT, preferred_element_type=jnp.float32).astype(jnp.bfloat16)
    values = lax.dot_general(wvt_ref[...], normed, NT, preferred_element_type=jnp.float32)
    index = lax.broadcasted_iota(jnp.int32, values.shape, 0)
    ones = (index == HD) | (index == HP + HD)
    return qk, jnp.where(ones, 1.0, values).astype(jnp.bfloat16)


def spread_kernel(table_ref, wqk_ref, wvt_ref):
    table = table_ref[...].astype(jnp.float32)
    width = table.shape[1]
    wide, narrow = jnp.zeros((LANES - HD, width)), jnp.zeros((HP - HD, width))
    pieces = [table[HD * index : HD * index + HD] for index in range(6)]
    wqk_ref[...] = jnp.concatenate(
        [pieces[0], wide, pieces[1], wide, pieces[3], wide, pieces[4], wide], axis=0
    ).astype(jnp.bfloat16)
    wvt_ref[...] = jnp.concatenate([pieces[2], narrow, pieces[5], narrow], axis=0).astype(jnp.bfloat16)


def early_kernel(*refs):
    pieces, (modulation_ref, wqk_ref, wvt_ref, qk_ref, vt_ref) = refs[:-5], refs[-5:]
    for index in range(0, len(pieces), 2):
        rows = jnp.concatenate([pieces[index][...], pieces[index + 1][...]], axis=0)
        qk, vt = triples_of(rows.astype(jnp.float32), modulation_ref, wqk_ref, wvt_ref)
        start = LANES * index
        qk_ref[start : start + 2 * LANES] = qk
        vt_ref[:, start : start + 2 * LANES] = vt


def frame_kernel(
    place_ref, below_ref, above_ref, one_ref, two_ref, three_ref, four_ref, qk_ref, vt_ref, modulation_ref,
    wqk_ref, wvt_ref, out_ref, qk_late_ref, vt_late_ref,
):
    groups = ((below_ref, above_ref), (three_ref, four_ref, one_ref, two_ref))
    for index, group in enumerate(groups):
        rows = jnp.concatenate([ref[...] for ref in group], axis=0).astype(jnp.float32)
        qk, vt = triples_of(rows, modulation_ref, wqk_ref, wvt_ref)
        start = 2 * LANES * index
        qk_late_ref[start : start + 2 * LANES] = qk
        vt_late_ref[:, start : start + 2 * LANES] = vt
    parts = ((qk_ref, vt_ref), (qk_late_ref, vt_late_ref))
    blocks = (
        ((qk_ref, 0), (qk_ref, 128)),
        ((qk_ref, 256), (qk_late_ref, 0)),
        ((qk_ref, 384), (qk_late_ref, 128)),
        ((qk_late_ref, 384), (qk_late_ref, 256)),
    )
    for number, block in enumerate(blocks):
        outs = []
        for head in range(2):
            column = 2 * LANES * head
            queries = jnp.concatenate(
                [ref[start : start + LANES, column : column + LANES] for ref, start in block], axis=0
            )
            scores = [
                lax.dot_general(
                    qk[:, column + LANES : column + 2 * LANES], queries, NT,
                    preferred_element_type=jnp.float32,
                )
                for qk, _ in parts
            ]
            largest = jnp.maximum(*[jnp.max(part, axis=0, keepdims=True) for part in scores])
            mixed = sum(
                jnp.dot(
                    vt[HP * head : HP * head + HP],
                    jnp.exp2((part - largest) * EXP2_SCALE).astype(jnp.bfloat16),
                    preferred_element_type=jnp.float32,
                )
                for part, (_, vt) in zip(scores, parts)
            )
            outs.append(mixed[:HD] / mixed[HD : HD + 1])
        both = jnp.concatenate(outs, axis=0).astype(jnp.bfloat16)
        for part in range(2):
            out_ref[place_ref[2 * number + part]] = both[:, part * LANES : (part + 1) * LANES]


def pack_kernel(parts_ref, out_ref):
    parts = parts_ref[...].astype(jnp.float32)
    rows = [parts[16 * (4 * zh + zl) : 16 * (4 * zh + zl) + 8] for zl in range(4) for zh in range(4)]
    rows += [parts[16 * (4 * zh + zl) + 8 : 16 * (4 * zh + zl) + 16] for zh in range(4) for zl in range(2)]
    out_ref[...] = jnp.concatenate(rows, axis=0).astype(jnp.bfloat16)


def middle_kernel(mixed_ref, tables_ref, tokens_ref, modulation_ref, out_ref, table_ref, sem):
    copy = pltpu.make_async_copy(tables_ref.at[pl.ds(0, 9), :, pl.ds(LANES, 64), :], table_ref, sem)
    copy.start()
    slots = [mixed_ref[2 * zh + core] for core in range(2) for zh in range(4)]
    mixed = jnp.concatenate(
        [slot[16 * number : 16 * number + 16] for number in range(9) for slot in slots], axis=0
    )
    copy.wait()
    table = table_ref[...].reshape(-1, table_ref.shape[-1])
    branch = lax.dot_general(mixed, table, TN, preferred_element_type=jnp.float32)
    out_ref[...] = (
        tokens_ref[...].astype(jnp.float32) + modulation_ref[0, 2:3] * branch
    ).astype(jnp.bfloat16)


def time_attention(positions, triples, mixed_ref, first):
    rows = triples.shape[1]
    one = lax.broadcasted_iota(jnp.int32, (rows, rows), 0) % positions
    two = lax.broadcasted_iota(jnp.int32, (rows, rows), 1) % positions
    same = one == two
    scores, values = [], []
    for head in range(4):
        triple = jnp.concatenate(
            [triples[LANES * part + 32 * head : LANES * part + 32 * head + 32] for part in range(7)], axis=0
        )
        queries = triple[:HD].astype(jnp.bfloat16)
        keys = triple[HD : 2 * HD].astype(jnp.bfloat16)
        values.append(jnp.concatenate([triple[2 * HD : 192], triple[200:]], axis=0).astype(jnp.bfloat16))
        part = lax.dot_general(keys, queries, TN, preferred_element_type=jnp.float32)
        scores.append(jnp.where(same, part, -1e30))
    raised = [
        jnp.exp2((part - jnp.max(part, axis=0, keepdims=True)) * EXP2_SCALE) for part in scores
    ]
    for head in range(4):
        total = jnp.sum(raised[head], axis=0, keepdims=True)
        mixed = jnp.dot(values[head], raised[head].astype(jnp.bfloat16), preferred_element_type=jnp.float32)
        mixed_ref[first + head] = mixed / total


def time_kernel(
    positions, middle_ref, tables_ref, out_table_ref, modulation_ref, out_ref, held_ref, mixed_ref, out_held_ref, sems
):
    rows, width = middle_ref.shape
    copies = [
        pltpu.make_async_copy(
            tables_ref.at[group, pl.ds(0, 7), pl.ds(0, LANES), :], held_ref.at[group], sems.at[group]
        )
        for group in range(4)
    ]
    copies.append(pltpu.make_async_copy(out_table_ref, out_held_ref, sems.at[4]))
    for copy in copies:
        copy.start()
    second = modulated(
        middle_ref[...].astype(jnp.float32), modulation_ref[1, 0:1], modulation_ref[1, 1:2]
    )
    for group in range(4):
        copies[group].wait()
        table = held_ref[group].reshape(7 * LANES, width)
        triples = lax.dot_general(table, second, NT, preferred_element_type=jnp.float32)
        time_attention(positions, triples, mixed_ref, 4 * group)
    copies[4].wait()
    mixed = mixed_ref[...].reshape(-1, rows).astype(jnp.bfloat16)
    branch = lax.dot_general(mixed, out_held_ref[...], TN, preferred_element_type=jnp.float32)
    out_ref[...] = (
        middle_ref[...].astype(jnp.float32) + modulation_ref[1, 2:3] * branch
    ).astype(jnp.bfloat16)


def rotation(count, by):
    return [(index, (index + by) % count) for index in range(count)]


SWAP = [(0, 1), (1, 0)]


def shards(tokens, frame_qkv, frame_out, time_qkv, time_out, modulation):
    tokens = tokens[0]
    rows, width = tokens.shape
    half = rows // 2
    zh, core = lax.axis_index("zh"), lax.axis_index("c")

    def along(array, axis, by):
        return lax.ppermute(array, axis, rotation(4, by))

    def swapped(array):
        return lax.ppermute(array, "c", SWAP)

    before, after = along(tokens, "zh", 1), along(tokens, "zh", 3)
    beside = swapped(tokens)
    far_top, far_bottom = along(before[:half], "zh", 1), along(after[half:], "zh", 3)
    early = [tokens, beside, before, after]
    late = [swapped(before), swapped(after), far_top, far_bottom, swapped(far_top), swapped(far_bottom)]
    spots = [zh, (zh + 3) % 4, (zh + 1) % 4, (zh + 2) % 4]
    place = jnp.stack(
        [spot * 2 + side for spot in spots for side in (core, 1 - core)]
    ).astype(jnp.int32)

    x, y, zl = lax.axis_index("x"), lax.axis_index("y"), lax.axis_index("zl")
    start = jnp.minimum(32 * (2 * y + core), 216 - 32) + 8 * zh
    time_part = lax.dynamic_slice_in_dim(time_qkv, start, 8, 0)
    start = 16 * jnp.minimum(4 * x + y, 8) + 8 * (zl % 2)
    out_part = lax.dynamic_slice_in_dim(frame_out, start, 8, 0)
    part = jnp.concatenate([time_part, out_part], axis=0)
    parts = lax.all_gather(part, ("zh", "zl"), axis=0, tiled=True)
    parts = pl.pallas_call(
        pack_kernel,
        out_shape=jax.ShapeDtypeStruct((4 * 32 + 4 * 16, width), parts.dtype),
        in_specs=[whole()],
        out_specs=whole(),
        compiler_params=params(),
        name="pack",
    )(parts)
    tables = lax.all_gather(parts, ("x", "y", "c"), axis=0)
    tables = tables.reshape(4, 8, 192, width)

    wqk, wvt = pl.pallas_call(
        spread_kernel,
        out_shape=(
            jax.ShapeDtypeStruct((4 * LANES, width), jnp.bfloat16),
            jax.ShapeDtypeStruct((2 * HP, width), jnp.bfloat16),
        ),
        in_specs=[whole()],
        out_specs=(whole(), whole()),
        compiler_params=params(),
        name="spread",
    )(frame_qkv.T)

    soon = rows * len(early)
    qk, vt = pl.pallas_call(
        early_kernel,
        out_shape=(
            jax.ShapeDtypeStruct((soon, 4 * LANES), jnp.bfloat16),
            jax.ShapeDtypeStruct((2 * HP, soon), jnp.bfloat16),
        ),
        in_specs=[whole()] * (len(early) + 3),
        out_specs=(whole(), whole()),
        compiler_params=params(),
        cost_estimate=pl.CostEstimate(flops=2 * 10**9, bytes_accessed=5 * 10**6, transcendentals=0),
        name="early_triples",
    )(*early, modulation, wqk, wvt)

    rest = 4 * rows
    mixed = pl.pallas_call(
        frame_kernel,
        out_shape=jax.ShapeDtypeStruct(((soon + rest) // LANES, 2 * HD, LANES), jnp.bfloat16),
        in_specs=[pl.BlockSpec(memory_space=pltpu.SMEM)] + [whole()] * 11,
        out_specs=whole(),
        scratch_shapes=[
            pltpu.VMEM((rest, 4 * LANES), jnp.bfloat16),
            pltpu.VMEM((2 * HP, rest), jnp.bfloat16),
        ],
        compiler_params=params(),
        name="frame_attention",
    )(place, *late, qk, vt, modulation, wqk, wvt)

    mixed = lax.all_to_all(mixed, ("zh", "c"), 0, 0, tiled=True)
    middle = pl.pallas_call(
        middle_kernel,
        out_shape=jax.ShapeDtypeStruct((rows, width), jnp.bfloat16),
        in_specs=[whole(), pl.BlockSpec(memory_space=pl.ANY), whole(), whole()],
        out_specs=whole(),
        scratch_shapes=[pltpu.VMEM((9, 2, 64, width), jnp.bfloat16), pltpu.SemaphoreType.DMA],
        compiler_params=params(),
        name="middle",
    )(mixed, tables.reshape(16, 2, 192, width), tokens, modulation)

    middle = lax.all_to_all(middle, ("x", "zl"), 0, 0, tiled=True)

    out = pl.pallas_call(
        functools.partial(time_kernel, rows // 16),
        out_shape=jax.ShapeDtypeStruct((rows, width), jnp.bfloat16),
        in_specs=[whole(), pl.BlockSpec(memory_space=pl.ANY), pl.BlockSpec(memory_space=pl.ANY), whole()],
        out_specs=whole(),
        scratch_shapes=[
            pltpu.VMEM((4, 7, LANES, width), jnp.bfloat16),
            pltpu.VMEM((16, HD, rows), jnp.float32),
            pltpu.VMEM((width, width), jnp.bfloat16),
            pltpu.SemaphoreType.DMA((5,)),
        ],
        compiler_params=params(),
        name="time_block",
    )(middle, tables, time_out, modulation)
    out = lax.all_to_all(out, ("x", "zl"), 0, 0, tiled=True)
    return out[None]


def solution(mesh):
    fine = Mesh(mesh.devices.reshape(4, 4, 4, 4, 2), ("y", "x", "zl", "zh", "c"))
    frames, space = ("y", "x", "zl"), ("zh", "c")
    placed = (
        P(frames, space, None),
        P(None, space),
        P(space, None),
        P(("x", "zl"), None),
        P(),
        P("y", None, None),
    )
    return jax.shard_map(
        shards,
        mesh=fine,
        in_specs=placed,
        out_specs=P(frames, space, None),
        check_vma=False,
    )
```

```python
import functools
import math

import jax
import jax.numpy as jnp
from jax import lax
from jax.experimental import pallas as pl
from jax.experimental.pallas import tpu as pltpu
from jax.sharding import Mesh
from jax.sharding import PartitionSpec as P

HD = 72
HP = 80
LANES = 128
EPS = 1e-06
EXP2_SCALE = HD ** (-0.5) * math.log2(math.e)
NT = (((1,), (1,)), ((), ()))
TN = (((0,), (0,)), ((), ()))


def params(mib=48):
    return pltpu.CompilerParams(vmem_limit_bytes=mib * 1024 * 1024)


def whole():
    return pl.BlockSpec(memory_space=pltpu.VMEM)


def modulated(values, offset, stretch):
    center = jnp.mean(values, axis=-1, keepdims=True)
    values = values - center
    spread = jnp.mean(values * values, axis=-1, keepdims=True)
    return (values * lax.rsqrt(spread + EPS) * (1.0 + stretch) + offset).astype(jnp.bfloat16)


def triples_of(rows, modulation_ref, wqk_ref, wvt_ref):
    normed = modulated(rows, modulation_ref[0, 0:1], modulation_ref[0, 1:2])
    qk = lax.dot_general(normed, wqk_ref[...], NT, preferred_element_type=jnp.float32).astype(jnp.bfloat16)
    values = lax.dot_general(wvt_ref[...], normed, NT, preferred_element_type=jnp.float32)
    index = lax.broadcasted_iota(jnp.int32, values.shape, 0)
    ones = (index == HD) | (index == HP + HD)
    return qk, jnp.where(ones, 1.0, values).astype(jnp.bfloat16)


def turn_kernel(below_ref, above_ref, top_ref, bottom_ref):
    half = top_ref.shape[0]
    top_ref[...] = below_ref[:half]
    bottom_ref[...] = above_ref[half:]


def spread_kernel(table_ref, wqk_ref, wvt_ref):
    table = table_ref[...].astype(jnp.float32)
    width = table.shape[1]
    wide, narrow = jnp.zeros((LANES - HD, width)), jnp.zeros((HP - HD, width))
    pieces = [table[HD * index : HD * index + HD] for index in range(6)]
    wqk_ref[...] = jnp.concatenate(
        [pieces[0], wide, pieces[1], wide, pieces[3], wide, pieces[4], wide], axis=0
    ).astype(jnp.bfloat16)
    wvt_ref[...] = jnp.concatenate([pieces[2], narrow, pieces[5], narrow], axis=0).astype(jnp.bfloat16)


def early_kernel(*refs):
    pieces, (modulation_ref, wqk_ref, wvt_ref, qk_ref, vt_ref) = refs[:-5], refs[-5:]
    for index in range(0, len(pieces), 2):
        rows = jnp.concatenate([pieces[index][...], pieces[index + 1][...]], axis=0)
        qk, vt = triples_of(rows.astype(jnp.float32), modulation_ref, wqk_ref, wvt_ref)
        start = LANES * index
        qk_ref[start : start + 2 * LANES] = qk
        vt_ref[:, start : start + 2 * LANES] = vt


def frame_kernel(
    place_ref, below_ref, above_ref, one_ref, two_ref, three_ref, four_ref, qk_ref, vt_ref, modulation_ref,
    wqk_ref, wvt_ref, out_ref, qk_late_ref, vt_late_ref,
):
    groups = ((below_ref, above_ref), (three_ref, four_ref, one_ref, two_ref))
    for index, group in enumerate(groups):
        rows = jnp.concatenate([ref[...] for ref in group], axis=0).astype(jnp.float32)
        qk, vt = triples_of(rows, modulation_ref, wqk_ref, wvt_ref)
        start = 2 * LANES * index
        qk_late_ref[start : start + 2 * LANES] = qk
        vt_late_ref[:, start : start + 2 * LANES] = vt
    parts = ((qk_ref, vt_ref), (qk_late_ref, vt_late_ref))
    blocks = (
        ((qk_ref, 0), (qk_ref, 128)),
        ((qk_ref, 256), (qk_late_ref, 0)),
        ((qk_ref, 384), (qk_late_ref, 128)),
        ((qk_late_ref, 384), (qk_late_ref, 256)),
    )
    for number, block in enumerate(blocks):
        outs = []
        for head in range(2):
            column = 2 * LANES * head
            queries = jnp.concatenate(
                [ref[start : start + LANES, column : column + LANES] for ref, start in block], axis=0
            )
            scores = [
                lax.dot_general(
                    qk[:, column + LANES : column + 2 * LANES], queries, NT,
                    preferred_element_type=jnp.float32,
                )
                for qk, _ in parts
            ]
            largest = jnp.maximum(*[jnp.max(part, axis=0, keepdims=True) for part in scores])
            mixed = sum(
                jnp.dot(
                    vt[HP * head : HP * head + HP],
                    jnp.exp2((part - largest) * EXP2_SCALE).astype(jnp.bfloat16),
                    preferred_element_type=jnp.float32,
                )
                for part, (_, vt) in zip(scores, parts)
            )
            outs.append(mixed[:HD] / mixed[HD : HD + 1])
        both = jnp.concatenate(outs, axis=0).astype(jnp.bfloat16)
        for part in range(2):
            out_ref[place_ref[2 * number + part]] = both[:, part * LANES : (part + 1) * LANES]


def pack_kernel(parts_ref, out_ref):
    parts = parts_ref[...].astype(jnp.float32)
    rows = [parts[16 * (4 * zh + zl) : 16 * (4 * zh + zl) + 8] for zl in range(4) for zh in range(4)]
    rows += [parts[16 * (4 * zh + zl) + 8 : 16 * (4 * zh + zl) + 16] for zh in range(4) for zl in range(2)]
    out_ref[...] = jnp.concatenate(rows, axis=0).astype(jnp.bfloat16)


def middle_kernel(mixed_ref, tables_ref, tokens_ref, modulation_ref, out_ref, table_ref, sem):
    copy = pltpu.make_async_copy(tables_ref.at[pl.ds(0, 9), :, pl.ds(LANES, 64), :], table_ref, sem)
    copy.start()
    slots = [mixed_ref[2 * zh + core] for core in range(2) for zh in range(4)]
    mixed = jnp.concatenate(
        [slot[16 * number : 16 * number + 16] for number in range(9) for slot in slots], axis=0
    )
    copy.wait()
    table = table_ref[...].reshape(-1, table_ref.shape[-1])
    branch = lax.dot_general(mixed, table, TN, preferred_element_type=jnp.float32)
    out_ref[...] = (
        tokens_ref[...].astype(jnp.float32) + modulation_ref[0, 2:3] * branch
    ).astype(jnp.bfloat16)


def time_attention(positions, triples, mixed_ref, first):
    rows = triples.shape[1]
    one = lax.broadcasted_iota(jnp.int32, (rows, rows), 0) % positions
    two = lax.broadcasted_iota(jnp.int32, (rows, rows), 1) % positions
    same = one == two
    scores, values = [], []
    for head in range(4):
        triple = jnp.concatenate(
            [triples[LANES * part + 32 * head : LANES * part + 32 * head + 32] for part in range(7)], axis=0
        )
        queries = triple[:HD].astype(jnp.bfloat16)
        keys = triple[HD : 2 * HD].astype(jnp.bfloat16)
        values.append(jnp.concatenate([triple[2 * HD : 192], triple[200:]], axis=0).astype(jnp.bfloat16))
        part = lax.dot_general(keys, queries, TN, preferred_element_type=jnp.float32)
        scores.append(jnp.where(same, part, -1e30))
    raised = [
        jnp.exp2((part - jnp.max(part, axis=0, keepdims=True)) * EXP2_SCALE) for part in scores
    ]
    for head in range(4):
        total = jnp.sum(raised[head], axis=0, keepdims=True)
        mixed = jnp.dot(values[head], raised[head].astype(jnp.bfloat16), preferred_element_type=jnp.float32)
        mixed_ref[first + head] = mixed / total


def time_kernel(
    positions, middle_ref, tables_ref, out_table_ref, modulation_ref, out_ref, held_ref, mixed_ref, out_held_ref, sems
):
    rows, width = middle_ref.shape
    copies = [
        pltpu.make_async_copy(
            tables_ref.at[group, pl.ds(0, 7), pl.ds(0, LANES), :], held_ref.at[group], sems.at[group]
        )
        for group in range(4)
    ]
    copies.append(pltpu.make_async_copy(out_table_ref, out_held_ref, sems.at[4]))
    for copy in copies:
        copy.start()
    second = modulated(
        middle_ref[...].astype(jnp.float32), modulation_ref[1, 0:1], modulation_ref[1, 1:2]
    )
    for group in range(4):
        copies[group].wait()
        table = held_ref[group].reshape(7 * LANES, width)
        triples = lax.dot_general(table, second, NT, preferred_element_type=jnp.float32)
        time_attention(positions, triples, mixed_ref, 4 * group)
    copies[4].wait()
    mixed = mixed_ref[...].reshape(-1, rows).astype(jnp.bfloat16)
    branch = lax.dot_general(mixed, out_held_ref[...], TN, preferred_element_type=jnp.float32)
    out_ref[...] = (
        middle_ref[...].astype(jnp.float32) + modulation_ref[1, 2:3] * branch
    ).astype(jnp.bfloat16)


def rotation(count, by):
    return [(index, (index + by) % count) for index in range(count)]


SWAP = [(0, 1), (1, 0)]


def shards(tokens, frame_qkv, frame_out, time_qkv, time_out, modulation):
    tokens = tokens[0]
    rows, width = tokens.shape
    half = rows // 2
    zh, core = lax.axis_index("zh"), lax.axis_index("c")

    def along(array, axis, by):
        return lax.ppermute(array, axis, rotation(4, by))

    def swapped(array):
        return lax.ppermute(array, "c", SWAP)

    before, after = along(tokens, "zh", 1), along(tokens, "zh", 3)
    beside = swapped(tokens)
    top, bottom = pl.pallas_call(
        turn_kernel,
        out_shape=(jax.ShapeDtypeStruct((half, width), tokens.dtype),) * 2,
        in_specs=[whole(), whole()],
        out_specs=(whole(),) * 2,
        compiler_params=params(16),
        name="turn",
    )(before, after)
    far_top, far_bottom = along(top, "zh", 1), along(bottom, "zh", 3)
    early = [tokens, beside, before, after]
    late = [swapped(before), swapped(after), far_top, far_bottom, swapped(far_top), swapped(far_bottom)]
    spots = [zh, (zh + 3) % 4, (zh + 1) % 4, (zh + 2) % 4]
    place = jnp.stack(
        [spot * 2 + side for spot in spots for side in (core, 1 - core)]
    ).astype(jnp.int32)

    x, y, zl = lax.axis_index("x"), lax.axis_index("y"), lax.axis_index("zl")
    start = jnp.minimum(32 * (2 * y + core), 216 - 32) + 8 * zh
    time_part = lax.dynamic_slice_in_dim(time_qkv, start, 8, 0)
    start = 16 * jnp.minimum(4 * x + y, 8) + 8 * (zl % 2)
    out_part = lax.dynamic_slice_in_dim(frame_out, start, 8, 0)
    part = jnp.concatenate([time_part, out_part], axis=0)
    parts = lax.all_gather(part, ("zh", "zl"), axis=0, tiled=True)
    parts = pl.pallas_call(
        pack_kernel,
        out_shape=jax.ShapeDtypeStruct((4 * 32 + 4 * 16, width), parts.dtype),
        in_specs=[whole()],
        out_specs=whole(),
        compiler_params=params(),
        name="pack",
    )(parts)
    tables = lax.all_gather(parts, ("x", "y", "c"), axis=0)
    tables = tables.reshape(4, 8, 192, width)

    wqk, wvt = pl.pallas_call(
        spread_kernel,
        out_shape=(
            jax.ShapeDtypeStruct((4 * LANES, width), jnp.bfloat16),
            jax.ShapeDtypeStruct((2 * HP, width), jnp.bfloat16),
        ),
        in_specs=[whole()],
        out_specs=(whole(), whole()),
        compiler_params=params(),
        name="spread",
    )(frame_qkv.T)

    soon = rows * len(early)
    qk, vt = pl.pallas_call(
        early_kernel,
        out_shape=(
            jax.ShapeDtypeStruct((soon, 4 * LANES), jnp.bfloat16),
            jax.ShapeDtypeStruct((2 * HP, soon), jnp.bfloat16),
        ),
        in_specs=[whole()] * (len(early) + 3),
        out_specs=(whole(), whole()),
        compiler_params=params(),
        cost_estimate=pl.CostEstimate(flops=2 * 10**9, bytes_accessed=5 * 10**6, transcendentals=0),
        name="early_triples",
    )(*early, modulation, wqk, wvt)

    rest = 4 * rows
    mixed = pl.pallas_call(
        frame_kernel,
        out_shape=jax.ShapeDtypeStruct(((soon + rest) // LANES, 2 * HD, LANES), jnp.bfloat16),
        in_specs=[pl.BlockSpec(memory_space=pltpu.SMEM)] + [whole()] * 11,
        out_specs=whole(),
        scratch_shapes=[
            pltpu.VMEM((rest, 4 * LANES), jnp.bfloat16),
            pltpu.VMEM((2 * HP, rest), jnp.bfloat16),
        ],
        compiler_params=params(),
        name="frame_attention",
    )(place, *late, qk, vt, modulation, wqk, wvt)

    mixed = lax.all_to_all(mixed, ("zh", "c"), 0, 0, tiled=True)
    middle = pl.pallas_call(
        middle_kernel,
        out_shape=jax.ShapeDtypeStruct((rows, width), jnp.bfloat16),
        in_specs=[whole(), pl.BlockSpec(memory_space=pl.ANY), whole(), whole()],
        out_specs=whole(),
        scratch_shapes=[pltpu.VMEM((9, 2, 64, width), jnp.bfloat16), pltpu.SemaphoreType.DMA],
        compiler_params=params(),
        name="middle",
    )(mixed, tables.reshape(16, 2, 192, width), tokens, modulation)

    middle = lax.all_to_all(middle, ("x", "zl"), 0, 0, tiled=True)

    out = pl.pallas_call(
        functools.partial(time_kernel, rows // 16),
        out_shape=jax.ShapeDtypeStruct((rows, width), jnp.bfloat16),
        in_specs=[whole(), pl.BlockSpec(memory_space=pl.ANY), pl.BlockSpec(memory_space=pl.ANY), whole()],
        out_specs=whole(),
        scratch_shapes=[
            pltpu.VMEM((4, 7, LANES, width), jnp.bfloat16),
            pltpu.VMEM((16, HD, rows), jnp.float32),
            pltpu.VMEM((width, width), jnp.bfloat16),
            pltpu.SemaphoreType.DMA((5,)),
        ],
        compiler_params=params(),
        name="time_block",
    )(middle, tables, time_out, modulation)
    out = lax.all_to_all(out, ("x", "zl"), 0, 0, tiled=True)
    return out[None]


def solution(mesh):
    fine = Mesh(mesh.devices.reshape(4, 4, 4, 4, 2), ("y", "x", "zl", "zh", "c"))
    frames, space = ("y", "x", "zl"), ("zh", "c")
    placed = (
        P(frames, space, None),
        P(None, space),
        P(space, None),
        P(("x", "zl"), None),
        P(),
        P("y", None, None),
    )
    return jax.shard_map(
        shards,
        mesh=fine,
        in_specs=placed,
        out_specs=P(frames, space, None),
        check_vma=False,
    )
```
